256 devices in a mesh: kv: 64 (over y, z_lo, x), req: 4 (over z_hi, core).
Axes of the slice: x: 4, y: 4, z: 8 (z_hi: 2, z_lo: 4; z = z_hi * 4 + z_lo), core: 2. Of those that a mesh axis runs over, the one named last changes fastest.
Arguments:
- q_nope: bfloat16 [2, 4, 128, 128], P(None, 'req', 'kv'), parts along dimension 1, may hold values from -6 to 6
- q_rope: bfloat16 [2, 4, 128, 64], P(None, 'req', 'kv'), parts along dimension 1, may hold values from -12 to 12
- uk_weight: bfloat16 [128, 128, 512], P('kv'), may hold values from -0.5 to 0.5
- uv_weight: bfloat16 [128, 512, 128], P('kv'), may hold values from -0.25 to 0.25
- out_weight: bfloat16 [16384, 7168], P('kv'), may hold values from -0.125 to 0.125
- cache: bfloat16 [4, 131072, 576], P('req', 'kv'), parts along dimension 0, may hold values from -12 to 12
- new_rows: bfloat16 [2, 4, 576], P(None, 'req'), parts along dimension 1, may hold values from -12 to 12
- context_len: int32 [4], P('req'), parts along dimension 0, may hold values from 32768 to 131070, as said below
Outputs:
- attended: bfloat16 [2, 4, 7168], P(None, 'req', 'kv'), parts along dimension 1
The draws below stay inside these ranges and needn't reach their ends.
There are 4 independent parts, one for each index of `req`. The reference program is written for one: setup_inputs(seed, part) draws one part's arguments, and reference() takes and returns one part's arrays. A program takes and returns all parts, laid end to end along the dimension named above; an argument that names none is the same for every part. Nothing has to cross between parts.
Inputs may be any that keep to these rules, and one draw needn't show every extreme that they name: `context_len`: each request has at least 32768 cached tokens; in every draw, over all request groups, the longest request has exactly 131070.
All inputs are finite; a program needn't handle non-finite values.
Results may differ from the reference program's by a relative error of at most 0.02.
Values may be sent and summed in bfloat16 or wider, within the bound.
A program may use at most 128 MiB of HBM per device.

```python
import jax
import jax.numpy as jnp
from jax import lax

D = 7168
H = 128
LAT = 512
ROPE = 64
NOPE = 128
VDIM = 128
REQS = 1
CTX_DEV = 2048
STEPS = 2
ROWS = 131072
WIDE = 576
N_KV = 64


def draw_q_rope(key, part):
    key = jax.random.fold_in(key, 23)
    noise_key = jax.random.fold_in(key, 0)
    values = jnp.clip(jax.random.normal(noise_key, (STEPS, REQS, H, ROPE), jnp.float32), -6.0, 6.0)
    return values.astype(jnp.bfloat16)


def draw_cache(key, part):
    key = jax.random.fold_in(key, 29)
    noise_key = jax.random.fold_in(key, 0)
    values = jnp.clip(jax.random.normal(noise_key, (REQS, ROWS, WIDE), jnp.float32), -6.0, 6.0)
    return values.astype(jnp.bfloat16)


def draw_context_len(key, part):
    key = jax.random.fold_in(key, 11)
    first, second, third = jax.random.split(key, 3)
    longest = ROWS - STEPS
    lengths = jax.random.randint(first, (REQS,), ROWS // 4, longest + 1)
    chosen = jax.random.randint(second, (), 0, REQS)
    holds = (part == 0) | jax.random.bernoulli(third, 0.25)
    marked = (jnp.arange(REQS) == chosen) & holds
    return jnp.where(marked, longest, lengths).astype(jnp.int32)


def with_spikes(result, stream_key, source, target, parts, factor):
    def block_of(axis_at):
        return (jnp.arange(result.shape[axis_at]) // (result.shape[axis_at] // parts)).reshape((-1,) + (1,) * (result.ndim - 1 - axis_at))

    near = jax.random.permutation(stream_key, parts)[block_of(target)]
    second = (block_of(target) + parts // 2) % parts
    return jnp.where((block_of(source) == near) | (block_of(source) == second), factor * result, result)


def block_scale(stream_key, dims, cuts, low, largest):
    def one(dim, blocks):
        draws = jax.random.uniform(jax.random.fold_in(jax.random.fold_in(stream_key, 6), dim), (blocks,), jnp.float32, low / len(cuts), largest / len(cuts))
        return jnp.repeat(jnp.exp(draws), dims[dim] // blocks).reshape((-1,) + (1,) * (len(dims) - dim - 1))

    level = one(*cuts[0])
    for cut in cuts[1:]:
        level = level * one(*cut)
    return level


def gaussian(rng, shape, deviation, most, cuts=(), held_as=jnp.bfloat16):
    entries = jax.random.normal(rng, shape, jnp.float32) * deviation
    if len(cuts) > 0:
        entries = block_scale(rng, shape, cuts, -0.22, 0.18) * entries
    return jnp.clip(entries, min=-most, max=most).astype(held_as)


def bell_draw_with(own_key, dims, width, bound, cuts, heavy, held_as=jnp.bfloat16):
    entries = width * jax.random.normal(own_key, dims, jnp.float32)
    if cuts:
        entries = entries * block_scale(own_key, dims, cuts, -0.22, 0.18)
    return jnp.clip(with_spikes(entries, jax.random.fold_in(own_key, 3), *heavy), -bound, bound).astype(held_as)


def setup_inputs(seed: int = 0, part: int = 0) -> dict:
    arg_keys = jax.random.split(jax.random.key(seed), 9)
    part_keys = jax.random.split(jax.random.fold_in(arg_keys[8], part), 9)
    return {
        "q_nope": gaussian(part_keys[0], (STEPS, REQS, H, NOPE), 1.0, 6.0, ((2, 64),)),
        "q_rope": draw_q_rope(jax.random.fold_in(jax.random.fold_in(arg_keys[8], part), 71), part),
        "uk_weight": gaussian(arg_keys[2], (H, NOPE, LAT), NOPE ** -0.5, 0.5, ((0, 64),)),
        "uv_weight": gaussian(arg_keys[3], (H, LAT, VDIM), LAT ** -0.5, 0.25, ((0, 64),)),
        "out_weight": bell_draw_with(arg_keys[4], (H * VDIM, D), (H * VDIM) ** -0.5, 0.125, ((0, 64),), (0, 1, 64, 4.0)),
        "cache": draw_cache(jax.random.fold_in(jax.random.fold_in(arg_keys[8], part), 71), part),
        "new_rows": gaussian(part_keys[6], (STEPS, REQS, WIDE), 2.0, 12.0),
        "context_len": draw_context_len(jax.random.fold_in(jax.random.fold_in(arg_keys[8], part), 71), part),
    }


def reference(q_nope, q_rope, uk_weight, uv_weight, out_weight, cache, new_rows, context_len):
    scale = (NOPE + ROPE) ** -0.5
    indices = jnp.arange(ROWS, dtype=jnp.int32)
    tokens = (indices % CTX_DEV) * N_KV + indices // CTX_DEV
    requests = jnp.arange(REQS, dtype=jnp.int32)
    results = []
    updated_cache = cache
    for step in range(STEPS):
        query_lat = jnp.einsum('bhn,hnl->bhl', q_nope[step].astype(jnp.float32), uk_weight.astype(jnp.float32)).astype(jnp.bfloat16)
        query = jnp.concatenate([query_lat, q_rope[step]], axis=-1)
        position = (context_len + step).astype(jnp.int32)
        target = ((position % N_KV) * CTX_DEV + position // N_KV).astype(jnp.int32)
        updated_cache = updated_cache.at[requests, target].set(new_rows[step])
        valid = tokens[None, :] < (position + 1)[:, None]

        def attend(items):
            one_query, one_cache, one_valid = items
            scores = jnp.dot(one_query, one_cache.T, preferred_element_type=jnp.float32) * scale
            scores = jnp.where(one_valid[None, :], scores, -jnp.inf)
            peak = jnp.max(scores, axis=-1, keepdims=True)
            expo = jnp.exp(scores - peak)
            total = jnp.sum(expo, axis=-1, keepdims=True)
            weights = expo.astype(jnp.bfloat16)
            summed = jnp.dot(weights, one_cache[:, :LAT], preferred_element_type=jnp.float32)
            return (summed / total).astype(jnp.bfloat16)

        head_latent = lax.map(attend, (query, updated_cache, valid))
        head_value = jnp.einsum('bhl,hlv->bhv', head_latent.astype(jnp.float32), uv_weight.astype(jnp.float32)).astype(jnp.bfloat16)
        flat = head_value.reshape(REQS, H * VDIM)
        results.append(jnp.dot(flat, out_weight, preferred_element_type=jnp.float32).astype(jnp.bfloat16))
    return jnp.stack(results, axis=0)
```

```python
import functools
import math

import jax
import jax.numpy as jnp
from jax import lax
from jax.experimental import pallas as pl
from jax.experimental.pallas import tpu as pltpu
from jax.sharding import PartitionSpec as P

MESH = pl.DeviceIdType.MESH
F32 = jnp.float32
BF16 = jnp.bfloat16

SIDE = 4
HOLD = 2
STEPS = 2
ROWS = HOLD * STEPS
LAT = 512
ROPE = 64
WIDE = LAT + ROPE
WIDE_PAD = 640
NEVER = -1e30

RING = [(dy, dx) for dy in range(SIDE) for dx in range(SIDE) if dy or dx]
RING.sort(key=lambda d: -(min(d[0], SIDE - d[0]) + min(d[1], SIDE - d[1])))
LINE = (3, 2, 1)


def split(value):
    high = value.astype(BF16).astype(F32)
    return high, (value - high).astype(BF16).astype(F32)


def with_stats(peak, total, rows):
    lane = lax.broadcasted_iota(jnp.int32, (rows, 128), 1)
    result = jnp.zeros((rows, 128), F32)
    for at, part in enumerate((*split(peak), *split(total))):
        result = jnp.where(lane == at, part, result)
    return result


def join(parts, pick, out_rows):
    stats = parts[:, LAT:].astype(F32).T
    peak = stats[0:1] + stats[1:2]
    total = stats[2:3] + stats[3:4]
    n = parts.shape[0]
    peaks = jnp.where(pick, jnp.broadcast_to(peak, (out_rows, n)), -3e38)
    top = jnp.max(peaks, axis=1, keepdims=True)
    factor = jnp.where(pick, jnp.exp2(peaks - top), 0.0)
    whole = jnp.sum(factor * total, axis=1, keepdims=True)
    high, low = split(factor)
    both = jnp.concatenate([high, low], axis=0).astype(BF16)
    summed = jnp.dot(both, parts[:, :LAT], preferred_element_type=F32)
    return summed[:out_rows] + summed[out_rows:], top, whole


def kernel(
    q_nope, q_rope, uk, uv, out_w, cache, new_rows, context, out,
    qn_v, qr_v, uk_v, uv_v, w_v, c_v, new_v, ctx_s, qx, zq, q_all, keys, scores, ob, rb, rb2, ts, tr,
    load_sem, send_sem, recv_sem,
):
    me = lax.axis_index("kv")
    y, z, x = me // 16, (me // 4) % 4, me % 4
    plane = y * 4 + x
    in_plane = [((y + dy) % 4, (x + dx) % 4) for dy, dx in RING]
    in_line = [(z + dz) % 4 for dz in LINE]

    def plane_id(peer):
        return {"kv": peer[0] * 16 + z * 4 + peer[1]}

    def line_id(peer):
        return {"kv": y * 16 + peer * 4 + x}

    barrier = pltpu.get_barrier_semaphore()
    for peer in in_plane:
        pl.semaphore_signal(barrier, inc=1, device_id=plane_id(peer), device_id_type=MESH)
    for peer in in_line:
        pl.semaphore_signal(barrier, inc=1, device_id=line_id(peer), device_id_type=MESH)

    loads = [
        pltpu.make_async_copy(src, dst, load_sem.at[k])
        for k, (src, dst) in enumerate(
            [(q_nope, qn_v), (q_rope, qr_v), (uk, uk_v), (context, ctx_s), (new_rows, new_v), (cache.at[0], c_v), (uv, uv_v), (out_w, w_v)]
        )
    ]
    for load in loads:
        load.start()
    l_qn, l_qr, l_uk, l_ctx, l_new, l_cache, l_uv, l_w = loads

    l_qn.wait()
    l_qr.wait()
    l_uk.wait()
    qx[...] = jnp.zeros((8, 128), F32)
    for step in range(STEPS):
        qx[step * 2 : step * 2 + 2, :] = qn_v[step, 0].astype(F32)
    lhs = qx[...].astype(BF16)
    even = lax.broadcasted_iota(jnp.int32, (8, 1), 0) % 2 == 0
    lat = jnp.where(
        even,
        jnp.dot(lhs, uk_v[0], preferred_element_type=F32),
        jnp.dot(lhs, uk_v[1], preferred_element_type=F32),
    )
    zq[z, 0:4, 0:LAT] = lat[0:4].astype(BF16).astype(F32)
    lane = lax.broadcasted_iota(jnp.int32, (2, ROPE), 1)
    for step in range(STEPS):
        flag = jnp.where(lane == step, 1.0, 0.0).astype(F32)
        zq[z, step * 2 : step * 2 + 2, LAT:] = jnp.concatenate(
            [qr_v[step, 0].astype(F32), flag], axis=1
        )

    pl.semaphore_wait(barrier, len(in_plane) + len(in_line))

    def remote(src, dst, phase, device):
        copy = pltpu.make_async_remote_copy(
            src_ref=src,
            dst_ref=dst,
            send_sem=send_sem.at[phase],
            recv_sem=recv_sem.at[phase],
            device_id=device,
            device_id_type=MESH,
        )
        copy.start()

    def take(ref, sem):
        pltpu.make_async_copy(ref, ref, sem).wait()

    mine = zq.at[z, pl.ds(0, 4)]
    for peer in in_line:
        remote(mine, mine, 0, line_id(peer))

    l_ctx.wait()
    l_new.wait()
    l_cache.wait()
    length = ctx_s[0]

    def prepare(k, _):
        base = pl.multiple_of(k * 256, 256)
        token = (lax.broadcasted_iota(jnp.int32, (256, 1), 0) + base) * 64 + me
        block = c_v[pl.ds(base, 256), :].astype(F32)
        for step in range(STEPS):
            block = jnp.where(token == length + step, new_v[step].astype(F32), block)
        lane = lax.broadcasted_iota(jnp.int32, (256, WIDE_PAD - WIDE), 1)
        mask = jnp.where((lane < STEPS) & (token > length + lane), NEVER, 0.0)
        keys[pl.ds(base, 256), :] = jnp.concatenate([block, mask], axis=1).astype(BF16)
        return 0

    lax.fori_loop(0, 4, prepare, 0)

    take(zq.at[pl.ds(0, 3), pl.ds(0, 4)], recv_sem.at[0])
    mine = q_all.at[pl.ds(pl.multiple_of(plane * 16, 16), 16)]
    mine[...] = jnp.concatenate([zq[k, 0:4, :] for k in range(4)], axis=0).astype(BF16)
    for peer in in_plane:
        remote(mine, mine, 1, plane_id(peer))
    lax.fori_loop(4, 8, prepare, 0)
    take(q_all.at[pl.ds(0, 240)], recv_sem.at[1])

    scale = math.log2(math.e) * (128 + ROPE) ** -0.5
    queries = q_all[...]
    peak = None
    for k in range(4):
        part = lax.dot_general(
            queries, keys[k * 512 : k * 512 + 512, :], (((1,), (1,)), ((), ())), preferred_element_type=F32
        )
        scores[:, k * 512 : k * 512 + 512] = part
        for j in range(4):
            tile = part[:, j * 128 : j * 128 + 128]
            peak = tile if peak is None else jnp.maximum(peak, tile)
    high, low = split(jnp.max(peak, axis=1, keepdims=True) * scale)
    peak = high + low
    total = jnp.zeros((256, 128), F32)
    value = jnp.zeros((256, LAT), F32)
    for k in range(4):
        expo = jnp.exp2(scores[:, k * 512 : k * 512 + 512] * scale - peak)
        for j in range(4):
            total = total + expo[:, j * 128 : j * 128 + 128]
        value = value + jnp.dot(
            expo.astype(BF16), keys[k * 512 : k * 512 + 512, 0:LAT], preferred_element_type=F32
        )
    ob[:, 0:LAT] = value.astype(BF16)
    ob[:, LAT:] = with_stats(peak, jnp.sum(total, axis=1, keepdims=True), 256).astype(BF16)

    mine = pl.ds(pl.multiple_of(plane * 16, 16), 16)
    for peer in in_plane:
        theirs = pl.ds(pl.multiple_of((peer[0] * 4 + peer[1]) * 16, 16), 16)
        remote(ob.at[theirs], rb.at[mine], 2, plane_id(peer))
    rb[mine, :] = ob[mine, :]
    take(rb.at[pl.ds(0, 240)], recv_sem.at[2])
    pick = (
        lax.broadcasted_iota(jnp.int32, (16, 256), 1) % 16
        == lax.broadcasted_iota(jnp.int32, (16, 256), 0)
    )
    summed, top, whole = join(rb[...], pick, 16)
    mine = rb2.at[pl.ds(pl.multiple_of(z * 16, 16), 16)]
    mine[...] = jnp.concatenate([summed, with_stats(top, whole, 16)], axis=1).astype(BF16)
    for peer in in_line:
        remote(mine, mine, 3, line_id(peer))
    l_uv.wait()
    l_w.wait()
    take(rb2.at[pl.ds(0, 48)], recv_sem.at[3])
    pick = lax.broadcasted_iota(jnp.int32, (8, 64), 1) % 16 == z * 4 + (
        lax.broadcasted_iota(jnp.int32, (8, 64), 0) % 4
    )
    summed, top, whole = join(rb2[...], pick, 8)
    latent = (summed / whole).astype(BF16)

    head_value = jnp.concatenate(
        [
            jnp.where(even, jnp.dot(latent, uv_v[0], preferred_element_type=F32), 0.0),
            jnp.where(even, 0.0, jnp.dot(latent, uv_v[1], preferred_element_type=F32)),
        ],
        axis=1,
    )
    pairs = head_value + pltpu.roll(head_value, 7, 0)
    first = lax.broadcasted_iota(jnp.int32, (8, 1), 0) == 0
    flat = jnp.where(first, pairs, pltpu.roll(pairs, 7, 0)).astype(BF16)
    for i in (4, 3, 5, 2, 6, 1, 7, 0):
        group = (me // 8 + i) % 8
        columns = pl.ds(pl.multiple_of(group * 896, 128), 896)
        term = jnp.dot(flat, w_v[:, columns], preferred_element_type=F32)
        for j in range(8):
            ts[group * 8 + j, :, 0:112] = term[:, j * 112 : j * 112 + 112]
        for j in range(8):
            peer = group * 8 + (me + j) % 8
            if i == 0 and j == 0:
                tr[me, 0:2, :] = ts[me, 0:2, :]
            else:
                remote(ts.at[peer, pl.ds(0, 2)], tr.at[me, pl.ds(0, 2)], 4, {"kv": peer})
    take(tr.at[pl.ds(0, 63), pl.ds(0, 2)], recv_sem.at[4])
    result = jnp.sum(tr[:, 0:2, :], axis=0)
    out[:, 0, :] = result[:, 0:112].astype(BF16)

    take(zq.at[pl.ds(0, 3), pl.ds(0, 4)], send_sem.at[0])
    take(q_all.at[pl.ds(0, 240)], send_sem.at[1])
    take(ob.at[pl.ds(0, 240)], send_sem.at[2])
    take(rb2.at[pl.ds(0, 48)], send_sem.at[3])
    take(ts.at[pl.ds(0, 63), pl.ds(0, 2)], send_sem.at[4])


def body(*args):
    any_space = pl.BlockSpec(memory_space=pl.ANY)
    return pl.pallas_call(
        kernel,
        out_shape=jax.ShapeDtypeStruct((STEPS, 1, 112), BF16),
        in_specs=[any_space] * 8,
        out_specs=pl.BlockSpec(memory_space=pltpu.VMEM),
        scratch_shapes=[
            pltpu.VMEM((2, 1, 2, 128), BF16),
            pltpu.VMEM((2, 1, 2, ROPE), BF16),
            pltpu.VMEM((2, 128, LAT), BF16),
            pltpu.VMEM((2, LAT, 128), BF16),
            pltpu.VMEM((256, 7168), BF16),
            pltpu.VMEM((2048, WIDE), BF16),
            pltpu.VMEM((2, 1, WIDE), BF16),
            pltpu.SMEM((1,), jnp.int32),
            pltpu.VMEM((8, 128), F32),
            pltpu.VMEM((4, 8, WIDE_PAD), F32),
            pltpu.VMEM((256, WIDE_PAD), BF16),
            pltpu.VMEM((2048, WIDE_PAD), BF16),
            pltpu.VMEM((256, 2048), F32),
            pltpu.VMEM((256, WIDE_PAD), BF16),
            pltpu.VMEM((256, WIDE_PAD), BF16),
            pltpu.VMEM((64, WIDE_PAD), BF16),
            pltpu.VMEM((64, 8, 128), F32),
            pltpu.VMEM((64, 8, 128), F32),
            pltpu.SemaphoreType.DMA((8,)),
            pltpu.SemaphoreType.DMA((5,)),
            pltpu.SemaphoreType.DMA((5,)),
        ],
        compiler_params=pltpu.CompilerParams(
            collective_id=0, has_side_effects=True, vmem_limit_bytes=48 << 20
        ),
    )(*args)


def solution(mesh):
    in_specs = (
        P(None, "req", "kv", None),
        P(None, "req", "kv", None),
        P("kv", None, None),
        P("kv", None, None),
        P("kv", None),
        P("req", "kv", None),
        P(None, "req", None),
        P("req"),
    )
    return jax.shard_map(body, mesh=mesh, in_specs=in_specs, out_specs=P(None, "req", "kv"), check_vma=False)
```

```python
import functools
import math

import jax
import jax.numpy as jnp
from jax import lax
from jax.experimental import pallas as pl
from jax.experimental.pallas import tpu as pltpu
from jax.sharding import PartitionSpec as P

MESH = pl.DeviceIdType.MESH
F32 = jnp.float32
BF16 = jnp.bfloat16

SIDE = 4
HOLD = 2
STEPS = 2
ROWS = HOLD * STEPS
LAT = 512
ROPE = 64
WIDE = LAT + ROPE
WIDE_PAD = 640
NEVER = -1e30

RING = [(dy, dx) for dy in range(SIDE) for dx in range(SIDE) if dy or dx]
RING.sort(key=lambda d: -(min(d[0], SIDE - d[0]) + min(d[1], SIDE - d[1])))
LINE = (3, 2, 1)


def split(value):
    high = value.astype(BF16).astype(F32)
    return high, (value - high).astype(BF16).astype(F32)


def with_stats(peak, total, rows):
    lane = lax.broadcasted_iota(jnp.int32, (rows, 128), 1)
    result = jnp.zeros((rows, 128), F32)
    for at, part in enumerate((*split(peak), *split(total))):
        result = jnp.where(lane == at, part, result)
    return result


def join(parts, pick, out_rows):
    stats = parts[:, LAT:].astype(F32).T
    peak = stats[0:1] + stats[1:2]
    total = stats[2:3] + stats[3:4]
    n = parts.shape[0]
    peaks = jnp.where(pick, jnp.broadcast_to(peak, (out_rows, n)), -3e38)
    top = jnp.max(peaks, axis=1, keepdims=True)
    factor = jnp.where(pick, jnp.exp2(peaks - top), 0.0)
    whole = jnp.sum(factor * total, axis=1, keepdims=True)
    high, low = split(factor)
    both = jnp.concatenate([high, low], axis=0).astype(BF16)
    summed = jnp.dot(both, parts[:, :LAT], preferred_element_type=F32)
    return summed[:out_rows] + summed[out_rows:], top, whole


def kernel(
    q_nope, q_rope, uk, uv, out_w, cache, new_rows, context, out,
    qn_v, qr_v, uk_v, uv_v, w_v, new_v, ctx_s, qx, zq, q_all, keys, scores, ob, rb, rb2, ts, tr,
    load_sem, send_sem, recv_sem,
):
    me = lax.axis_index("kv")
    y, z, x = me // 16, (me // 4) % 4, me % 4
    plane = y * 4 + x
    in_plane = [((y + dy) % 4, (x + dx) % 4) for dy, dx in RING]
    in_line = [(z + dz) % 4 for dz in LINE]

    def plane_id(peer):
        return {"kv": peer[0] * 16 + z * 4 + peer[1]}

    def line_id(peer):
        return {"kv": y * 16 + peer * 4 + x}

    barrier = pltpu.get_barrier_semaphore()
    for peer in in_plane:
        pl.semaphore_signal(barrier, inc=1, device_id=plane_id(peer), device_id_type=MESH)
    for peer in in_line:
        pl.semaphore_signal(barrier, inc=1, device_id=line_id(peer), device_id_type=MESH)

    loads = [
        pltpu.make_async_copy(src, dst, load_sem.at[k])
        for k, (src, dst) in enumerate(
            [(q_nope, qn_v), (q_rope, qr_v), (uk, uk_v), (context, ctx_s), (new_rows, new_v), (cache.at[0], keys.at[pl.ds(0, WIDE)]), (uv, uv_v), (out_w, w_v)]
        )
    ]
    for load in loads:
        load.start()
    l_qn, l_qr, l_uk, l_ctx, l_new, l_cache, l_uv, l_w = loads

    l_qn.wait()
    l_qr.wait()
    l_uk.wait()
    qx[...] = jnp.zeros((8, 128), F32)
    for step in range(STEPS):
        qx[step * 2 : step * 2 + 2, :] = qn_v[step, 0].astype(F32)
    lhs = qx[...].astype(BF16)
    even = lax.broadcasted_iota(jnp.int32, (8, 1), 0) % 2 == 0
    lat = jnp.where(
        even,
        jnp.dot(lhs, uk_v[0], preferred_element_type=F32),
        jnp.dot(lhs, uk_v[1], preferred_element_type=F32),
    )
    zq[z, 0:4, 0:LAT] = lat[0:4].astype(BF16).astype(F32)
    lane = lax.broadcasted_iota(jnp.int32, (2, ROPE), 1)
    for step in range(STEPS):
        flag = jnp.where(lane == step, 1.0, 0.0).astype(F32)
        zq[z, step * 2 : step * 2 + 2, LAT:] = jnp.concatenate(
            [qr_v[step, 0].astype(F32), flag], axis=1
        )

    pl.semaphore_wait(barrier, len(in_plane) + len(in_line))

    def remote(src, dst, phase, device):
        copy = pltpu.make_async_remote_copy(
            src_ref=src,
            dst_ref=dst,
            send_sem=send_sem.at[phase],
            recv_sem=recv_sem.at[phase],
            device_id=device,
            device_id_type=MESH,
        )
        copy.start()

    def take(ref, sem):
        pltpu.make_async_copy(ref, ref, sem).wait()

    mine = zq.at[z, pl.ds(0, 4)]
    for peer in in_line:
        remote(mine, mine, 0, line_id(peer))

    l_ctx.wait()
    l_new.wait()
    l_cache.wait()
    length = ctx_s[0]
    rows = jnp.concatenate([new_v[0].astype(F32), jnp.zeros((STEPS, WIDE_PAD - WIDE), F32)], axis=1)
    appended = jnp.concatenate([rows, jnp.zeros((8 - STEPS, WIDE_PAD), F32)], axis=0).T
    row = lax.broadcasted_iota(jnp.int32, (WIDE_PAD - WIDE, 1), 0)

    def prepare(k, _):
        here = pl.ds(pl.multiple_of(k * 256, 256), 256)
        token = (lax.broadcasted_iota(jnp.int32, (1, 256), 1) + k * 256) * 64 + me
        block = keys[0:WIDE, here].astype(F32)
        for step in range(STEPS):
            block = jnp.where(token == length + step, appended[0:WIDE, step : step + 1], block)
        keys[0:WIDE, here] = block.astype(BF16)
        mask = jnp.where((row < STEPS) & (token > length + row), NEVER, 0.0)
        keys[WIDE:, here] = mask.astype(BF16)
        return 0

    lax.fori_loop(0, 4, prepare, 0)

    take(zq.at[pl.ds(0, 3), pl.ds(0, 4)], recv_sem.at[0])
    mine = q_all.at[pl.ds(pl.multiple_of(plane * 16, 16), 16)]
    mine[...] = jnp.concatenate([zq[k, 0:4, :] for k in range(4)], axis=0).astype(BF16)
    for peer in in_plane:
        remote(mine, mine, 1, plane_id(peer))
    lax.fori_loop(4, 8, prepare, 0)
    take(q_all.at[pl.ds(0, 240)], recv_sem.at[1])

    scale = math.log2(math.e) * (128 + ROPE) ** -0.5
    queries = q_all[...]
    peak = None
    for k in range(4):
        part = jnp.dot(queries, keys[:, k * 512 : k * 512 + 512], preferred_element_type=F32)
        scores[:, k * 512 : k * 512 + 512] = part
        for j in range(4):
            tile = part[:, j * 128 : j * 128 + 128]
            peak = tile if peak is None else jnp.maximum(peak, tile)
    high, low = split(jnp.max(peak, axis=1, keepdims=True) * scale)
    peak = high + low
    total = jnp.zeros((256, 128), F32)
    value = jnp.zeros((256, LAT), F32)
    for k in range(4):
        expo = jnp.exp2(scores[:, k * 512 : k * 512 + 512] * scale - peak)
        for j in range(4):
            total = total + expo[:, j * 128 : j * 128 + 128]
        value = value + lax.dot_general(
            expo.astype(BF16), keys[0:LAT, k * 512 : k * 512 + 512], (((1,), (1,)), ((), ())), preferred_element_type=F32
        )
    ob[:, 0:LAT] = value.astype(BF16)
    ob[:, LAT:] = with_stats(peak, jnp.sum(total, axis=1, keepdims=True), 256).astype(BF16)

    mine = pl.ds(pl.multiple_of(plane * 16, 16), 16)
    for peer in in_plane:
        theirs = pl.ds(pl.multiple_of((peer[0] * 4 + peer[1]) * 16, 16), 16)
        remote(ob.at[theirs], rb.at[mine], 2, plane_id(peer))
    rb[mine, :] = ob[mine, :]
    take(rb.at[pl.ds(0, 240)], recv_sem.at[2])
    pick = (
        lax.broadcasted_iota(jnp.int32, (16, 256), 1) % 16
        == lax.broadcasted_iota(jnp.int32, (16, 256), 0)
    )
    summed, top, whole = join(rb[...], pick, 16)
    mine = rb2.at[pl.ds(pl.multiple_of(z * 16, 16), 16)]
    mine[...] = jnp.concatenate([summed, with_stats(top, whole, 16)], axis=1).astype(BF16)
    for peer in in_line:
        remote(mine, mine, 3, line_id(peer))
    l_uv.wait()
    l_w.wait()
    take(rb2.at[pl.ds(0, 48)], recv_sem.at[3])
    pick = lax.broadcasted_iota(jnp.int32, (8, 64), 1) % 16 == z * 4 + (
        lax.broadcasted_iota(jnp.int32, (8, 64), 0) % 4
    )
    summed, top, whole = join(rb2[...], pick, 8)
    latent = (summed / whole).astype(BF16)

    head_value = jnp.concatenate(
        [
            jnp.where(even, jnp.dot(latent, uv_v[0], preferred_element_type=F32), 0.0),
            jnp.where(even, 0.0, jnp.dot(latent, uv_v[1], preferred_element_type=F32)),
        ],
        axis=1,
    )
    pairs = head_value + pltpu.roll(head_value, 7, 0)
    first = lax.broadcasted_iota(jnp.int32, (8, 1), 0) == 0
    flat = jnp.where(first, pairs, pltpu.roll(pairs, 7, 0)).astype(BF16)
    for i in (4, 3, 5, 2, 6, 1, 7, 0):
        group = (me // 8 + i) % 8
        columns = pl.ds(pl.multiple_of(group * 896, 128), 896)
        term = jnp.dot(flat, w_v[:, columns], preferred_element_type=F32)
        for j in range(8):
            ts[group * 8 + j, :, 0:112] = term[:, j * 112 : j * 112 + 112]
        for j in range(8):
            peer = group * 8 + (me + j) % 8
            if i == 0 and j == 0:
                tr[me, 0:2, :] = ts[me, 0:2, :]
            else:
                remote(ts.at[peer, pl.ds(0, 2)], tr.at[me, pl.ds(0, 2)], 4, {"kv": peer})
    take(tr.at[pl.ds(0, 63), pl.ds(0, 2)], recv_sem.at[4])
    result = jnp.sum(tr[:, 0:2, :], axis=0)
    out[0] = result[:, 0:112].astype(BF16)

    take(zq.at[pl.ds(0, 3), pl.ds(0, 4)], send_sem.at[0])
    take(q_all.at[pl.ds(0, 240)], send_sem.at[1])
    take(ob.at[pl.ds(0, 240)], send_sem.at[2])
    take(rb2.at[pl.ds(0, 48)], send_sem.at[3])
    take(ts.at[pl.ds(0, 63), pl.ds(0, 2)], send_sem.at[4])


def body(q_nope, q_rope, uk, uv, out_w, cache, new_rows, context):
    hbm = pl.BlockSpec(memory_space=pltpu.HBM)
    result = pl.pallas_call(
        kernel,
        out_shape=pltpu.VMEM((1, STEPS, 112), BF16),
        in_specs=[hbm] * 8,
        out_specs=pl.BlockSpec(memory_space=pltpu.VMEM),
        scratch_shapes=[
            pltpu.VMEM((2, 1, 2, 128), BF16),
            pltpu.VMEM((2, 1, 2, ROPE), BF16),
            pltpu.VMEM((2, 128, LAT), BF16),
            pltpu.VMEM((2, LAT, 128), BF16),
            pltpu.VMEM((256, 7168), BF16),
            pltpu.VMEM((1, 2, WIDE), BF16),
            pltpu.SMEM((1,), jnp.int32),
            pltpu.VMEM((8, 128), F32),
            pltpu.VMEM((4, 8, WIDE_PAD), F32),
            pltpu.VMEM((256, WIDE_PAD), BF16),
            pltpu.VMEM((WIDE_PAD, 2048), BF16),
            pltpu.VMEM((256, 2048), F32),
            pltpu.VMEM((256, WIDE_PAD), BF16),
            pltpu.VMEM((256, WIDE_PAD), BF16),
            pltpu.VMEM((64, WIDE_PAD), BF16),
            pltpu.VMEM((64, 8, 128), F32),
            pltpu.VMEM((64, 8, 128), F32),
            pltpu.SemaphoreType.DMA((8,)),
            pltpu.SemaphoreType.DMA((5,)),
            pltpu.SemaphoreType.DMA((5,)),
        ],
        compiler_params=pltpu.CompilerParams(
            collective_id=0, has_side_effects=True, vmem_limit_bytes=60 << 20
        ),
    )(q_nope, q_rope, uk, uv, out_w, jnp.swapaxes(cache, 1, 2), jnp.swapaxes(new_rows, 0, 1), context)
    return jnp.swapaxes(result, 0, 1)


def solution(mesh):
    in_specs = (
        P(None, "req", "kv", None),
        P(None, "req", "kv", None),
        P("kv", None, None),
        P("kv", None, None),
        P("kv", None),
        P("req", "kv", None),
        P(None, "req", None),
        P("req"),
    )
    return jax.shard_map(body, mesh=mesh, in_specs=in_specs, out_specs=P(None, "req", "kv"), check_vma=False)
```

```python
import functools
import math

import jax
import jax.numpy as jnp
from jax import lax
from jax.experimental import pallas as pl
from jax.experimental.pallas import tpu as pltpu
from jax.sharding import PartitionSpec as P

MESH = pl.DeviceIdType.MESH
F32 = jnp.float32
BF16 = jnp.bfloat16

SIDE = 4
HOLD = 2
STEPS = 2
ROWS = HOLD * STEPS
LAT = 512
ROPE = 64
WIDE = LAT + ROPE
WIDE_PAD = 640
NEVER = -1e30
SENT = 18

RING = [(dy, dx) for dy in range(SIDE) for dx in range(SIDE) if dy or dx]
RING.sort(key=lambda d: -(min(d[0], SIDE - d[0]) + min(d[1], SIDE - d[1])))
LINE = (3, 2, 1)


def split(value):
    high = value.astype(BF16).astype(F32)
    return high, (value - high).astype(BF16).astype(F32)


def with_stats(peak, total, rows):
    lane = lax.broadcasted_iota(jnp.int32, (rows, 128), 1)
    row = lax.broadcasted_iota(jnp.int32, (rows, 128), 0) % ROWS
    result = jnp.zeros((rows, 128), F32)
    for at, part in enumerate((*split(peak), *split(total))):
        result = jnp.where(lane == row + at * ROWS, part, result)
    return result


def kernel(
    q_nope, q_rope, uk, uv, out_w, cache, new_rows, context, out,
    qn_v, qr_v, uk_v, uv_v, w_v, new_v, ctx_s, qx, zq, q_all, keys, scores, vals, stats, ob, rb, spread, ts, tr,
    load_sem, send_sem, recv_sem,
):
    me = lax.axis_index("kv")
    y, z, x = me // 16, (me // 4) % 4, me % 4
    plane = y * 4 + x
    in_plane = [((y + dy) % 4, (x + dx) % 4) for dy, dx in RING]
    in_line = [(z + dz) % 4 for dz in LINE]

    def plane_id(peer):
        return {"kv": peer[0] * 16 + z * 4 + peer[1]}

    def line_id(peer):
        return {"kv": y * 16 + peer * 4 + x}

    barrier = pltpu.get_barrier_semaphore()
    for peer in in_plane:
        pl.semaphore_signal(barrier, inc=1, device_id=plane_id(peer), device_id_type=MESH)
    for peer in in_line:
        pl.semaphore_signal(barrier, inc=1, device_id=line_id(peer), device_id_type=MESH)

    loads = [
        pltpu.make_async_copy(src, dst, load_sem.at[k])
        for k, (src, dst) in enumerate(
            [(q_nope, qn_v), (q_rope, qr_v), (uk, uk_v), (context, ctx_s), (new_rows, new_v), (cache.at[0], keys.at[pl.ds(0, WIDE)]), (uv, uv_v), (out_w, w_v)]
        )
    ]
    for load in loads:
        load.start()
    l_qn, l_qr, l_uk, l_ctx, l_new, l_cache, l_uv, l_w = loads

    l_qn.wait()
    l_qr.wait()
    l_uk.wait()
    qx[...] = jnp.zeros((8, 128), F32)
    for step in range(STEPS):
        qx[step * 2 : step * 2 + 2, :] = qn_v[step, 0].astype(F32)
    lhs = qx[...].astype(BF16)
    even = lax.broadcasted_iota(jnp.int32, (8, 1), 0) % 2 == 0
    lat = jnp.where(
        even,
        jnp.dot(lhs, uk_v[0], preferred_element_type=F32),
        jnp.dot(lhs, uk_v[1], preferred_element_type=F32),
    )
    zq[z, 0:4, 0:LAT] = lat[0:4].astype(BF16).astype(F32)
    lane = lax.broadcasted_iota(jnp.int32, (2, ROPE), 1)
    for step in range(STEPS):
        flag = jnp.where(lane == step, 1.0, 0.0).astype(F32)
        zq[z, step * 2 : step * 2 + 2, LAT:] = jnp.concatenate(
            [qr_v[step, 0].astype(F32), flag], axis=1
        )

    pl.semaphore_wait(barrier, len(in_plane) + len(in_line))

    def remote(src, dst, phase, device):
        copy = pltpu.make_async_remote_copy(
            src_ref=src,
            dst_ref=dst,
            send_sem=send_sem.at[phase],
            recv_sem=recv_sem.at[phase],
            device_id=device,
            device_id_type=MESH,
        )
        copy.start()

    def take(ref, sem):
        pltpu.make_async_copy(ref, ref, sem).wait()

    mine = zq.at[z, pl.ds(0, 4)]
    for peer in in_line:
        remote(mine, mine, 0, line_id(peer))

    l_ctx.wait()
    l_new.wait()
    l_cache.wait()
    length = ctx_s[0]
    rows = jnp.concatenate([new_v[0].astype(F32), jnp.zeros((STEPS, WIDE_PAD - WIDE), F32)], axis=1)
    appended = jnp.concatenate([rows, jnp.zeros((8 - STEPS, WIDE_PAD), F32)], axis=0).T
    row = lax.broadcasted_iota(jnp.int32, (WIDE_PAD - WIDE, 1), 0)

    def prepare(k, _):
        here = pl.ds(pl.multiple_of(k * 256, 256), 256)
        token = (lax.broadcasted_iota(jnp.int32, (1, 256), 1) + k * 256) * 64 + me
        block = keys[0:WIDE, here].astype(F32)
        for step in range(STEPS):
            block = jnp.where(token == length + step, appended[0:WIDE, step : step + 1], block)
        keys[0:WIDE, here] = block.astype(BF16)
        mask = jnp.where((row < STEPS) & (token > length + row), NEVER, 0.0)
        keys[WIDE:, here] = mask.astype(BF16)
        return 0

    lax.fori_loop(0, 4, prepare, 0)

    take(zq.at[pl.ds(0, 3), pl.ds(0, 4)], recv_sem.at[0])
    mine = q_all.at[pl.ds(pl.multiple_of(plane * 16, 16), 16)]
    mine[...] = jnp.concatenate([zq[k, 0:4, :] for k in range(4)], axis=0).astype(BF16)
    for peer in in_plane:
        remote(mine, mine, 1, plane_id(peer))
    lax.fori_loop(4, 8, prepare, 0)
    column = lax.broadcasted_iota(jnp.int32, (128, 1024), 1) // 16
    place = lax.broadcasted_iota(jnp.int32, (128, 1024), 0)
    spread[...] = jnp.where(column == place, 1.0, 0.0).astype(BF16)
    take(q_all.at[pl.ds(0, 240)], recv_sem.at[1])

    scale = math.log2(math.e) * (128 + ROPE) ** -0.5
    queries = q_all[...]
    peak = None
    for k in range(4):
        part = jnp.dot(queries, keys[:, k * 512 : k * 512 + 512], preferred_element_type=F32)
        scores[:, k * 512 : k * 512 + 512] = part
        for j in range(4):
            tile = part[:, j * 128 : j * 128 + 128]
            peak = tile if peak is None else jnp.maximum(peak, tile)
    high, low = split(jnp.max(peak, axis=1, keepdims=True) * scale)
    peak = high + low
    total = jnp.zeros((256, 128), F32)
    value = jnp.zeros((256, LAT), F32)
    for k in range(4):
        expo = jnp.exp2(scores[:, k * 512 : k * 512 + 512] * scale - peak)
        for j in range(4):
            total = total + expo[:, j * 128 : j * 128 + 128]
        value = value + lax.dot_general(
            expo.astype(BF16), keys[0:LAT, k * 512 : k * 512 + 512], (((1,), (1,)), ((), ())), preferred_element_type=F32
        )
    vals[...] = value
    stats[...] = with_stats(peak, jnp.sum(total, axis=1, keepdims=True), 256)

    low_half = lax.broadcasted_iota(jnp.int32, (8, 1), 0) < 4

    def halves(left, right):
        return (
            jnp.where(low_half, left, pltpu.roll(right, 4, 0)),
            jnp.where(low_half, pltpu.roll(left, 4, 0), right),
        )

    own_pair = z // 2
    for z_pair in (1 - own_pair, own_pair):
        for dy, dx in (*RING, (0, 0)):
            to_y, to_x = (y + dy) % 4, (x + dx) % 4
            eight = pl.ds(pl.multiple_of(((to_y * 4 + to_x) * 2 + z_pair) * 8, 8), 8)
            quarters = [vals[eight, k * 128 : k * 128 + 128] for k in range(4)]
            first, second = zip(halves(*quarters[:2]), halves(*quarters[2:]))
            note = stats[eight, :]
            note = note + pltpu.roll(note, 1, 0)
            note = note + pltpu.roll(note, 2, 0)
            for j, (rows, shift) in enumerate(((first, 5), (second, 1))):
                peer = to_y * 16 + (z_pair * 2 + j) * 4 + to_x
                ob[peer, 0:16, :] = jnp.concatenate(rows, axis=0).astype(BF16)
                moved = pltpu.roll(note, shift, 0)
                ob[peer, 16:32, :] = jnp.concatenate([moved, moved], axis=0).astype(BF16)
            for j in (1, 0):
                peer = to_y * 16 + (z_pair * 2 + (z + j) % 2) * 4 + to_x
                if z_pair is own_pair and dy == 0 and dx == 0 and j == 0:
                    rb[me] = ob[me]
                else:
                    remote(ob.at[peer, pl.ds(0, SENT)], rb.at[me, pl.ds(0, SENT)], 2, {"kv": peer})
    l_uv.wait()
    l_w.wait()
    take(rb.at[pl.ds(0, 63), pl.ds(0, SENT)], recv_sem.at[2])
    notes = jnp.concatenate(
        [rb[k, 16:18, :].astype(F32)[0:1] for k in range(64)] + [jnp.zeros((64, 128), F32)], axis=0
    ).T
    known = lax.broadcasted_iota(jnp.int32, (ROWS, 128), 1) < 64
    peak = jnp.where(known, notes[0:4] + notes[4:8], -3e38)
    factor = jnp.where(known, jnp.exp2(peak - jnp.max(peak, axis=1, keepdims=True)), 0.0)
    whole = jnp.sum(factor * (notes[8:12] + notes[12:16]), axis=1, keepdims=True)
    factor = factor / whole
    factor = jnp.concatenate([factor, factor], axis=0).astype(BF16)
    factor = jnp.dot(factor, spread[...], preferred_element_type=F32)
    column = lax.broadcasted_iota(jnp.int32, (16, 1024), 1) % 16
    place = lax.broadcasted_iota(jnp.int32, (16, 1024), 0)
    factor = jnp.where(column == place, jnp.concatenate([factor, factor], axis=0), 0.0).astype(BF16)
    joined = jnp.dot(
        factor, rb[:, 0:16, :].reshape(1024, 128), preferred_element_type=F32
    )
    top, bottom = joined[0:8], joined[8:16]
    latent = jnp.concatenate(
        [top, pltpu.roll(top, 4, 0), bottom, pltpu.roll(bottom, 4, 0)], axis=1
    ).astype(BF16)

    head_value = jnp.concatenate(
        [
            jnp.where(even, jnp.dot(latent, uv_v[0], preferred_element_type=F32), 0.0),
            jnp.where(even, 0.0, jnp.dot(latent, uv_v[1], preferred_element_type=F32)),
        ],
        axis=1,
    )
    pairs = head_value + pltpu.roll(head_value, 7, 0)
    first = lax.broadcasted_iota(jnp.int32, (8, 1), 0) == 0
    flat = jnp.where(first, pairs, pltpu.roll(pairs, 7, 0)).astype(BF16)
    for i in (4, 3, 5, 2, 6, 1, 7, 0):
        group = (me // 8 + i) % 8
        columns = pl.ds(pl.multiple_of(group * 896, 128), 896)
        term = jnp.dot(flat, w_v[:, columns], preferred_element_type=F32)
        for j in range(8):
            ts[group * 8 + j, :, 0:112] = term[:, j * 112 : j * 112 + 112]
        for j in range(8):
            peer = group * 8 + (me + j) % 8
            if i == 0 and j == 0:
                tr[me, 0:2, :] = ts[me, 0:2, :]
            else:
                remote(ts.at[peer, pl.ds(0, 2)], tr.at[me, pl.ds(0, 2)], 3, {"kv": peer})
    take(tr.at[pl.ds(0, 63), pl.ds(0, 2)], recv_sem.at[3])
    result = jnp.sum(tr[:, 0:2, :], axis=0)
    out[0] = result[:, 0:112].astype(BF16)

    take(zq.at[pl.ds(0, 3), pl.ds(0, 4)], send_sem.at[0])
    take(q_all.at[pl.ds(0, 240)], send_sem.at[1])
    take(ob.at[pl.ds(0, 63), pl.ds(0, SENT)], send_sem.at[2])
    take(ts.at[pl.ds(0, 63), pl.ds(0, 2)], send_sem.at[3])


def body(q_nope, q_rope, uk, uv, out_w, cache, new_rows, context):
    hbm = pl.BlockSpec(memory_space=pltpu.HBM)
    result = pl.pallas_call(
        kernel,
        out_shape=pltpu.VMEM((1, STEPS, 112), BF16),
        in_specs=[hbm] * 8,
        out_specs=pl.BlockSpec(memory_space=pltpu.VMEM),
        scratch_shapes=[
            pltpu.VMEM((2, 1, 2, 128), BF16),
            pltpu.VMEM((2, 1, 2, ROPE), BF16),
            pltpu.VMEM((2, 128, LAT), BF16),
            pltpu.VMEM((2, LAT, 128), BF16),
            pltpu.VMEM((256, 7168), BF16),
            pltpu.VMEM((1, 2, WIDE), BF16),
            pltpu.SMEM((1,), jnp.int32),
            pltpu.VMEM((8, 128), F32),
            pltpu.VMEM((4, 8, WIDE_PAD), F32),
            pltpu.VMEM((256, WIDE_PAD), BF16),
            pltpu.VMEM((WIDE_PAD, 2048), BF16),
            pltpu.VMEM((256, 2048), F32),
            pltpu.VMEM((256, LAT), F32),
            pltpu.VMEM((256, 128), F32),
            pltpu.VMEM((64, 32, 128), BF16),
            pltpu.VMEM((64, 32, 128), BF16),
            pltpu.VMEM((128, 1024), BF16),
            pltpu.VMEM((64, 8, 128), F32),
            pltpu.VMEM((64, 8, 128), F32),
            pltpu.SemaphoreType.DMA((8,)),
            pltpu.SemaphoreType.DMA((4,)),
            pltpu.SemaphoreType.DMA((4,)),
        ],
        compiler_params=pltpu.CompilerParams(
            collective_id=0, has_side_effects=True, vmem_limit_bytes=60 << 20
        ),
    )(q_nope, q_rope, uk, uv, out_w, jnp.swapaxes(cache, 1, 2), jnp.swapaxes(new_rows, 0, 1), context)
    return jnp.swapaxes(result, 0, 1)


def solution(mesh):
    in_specs = (
        P(None, "req", "kv", None),
        P(None, "req", "kv", None),
        P("kv", None, None),
        P("kv", None, None),
        P("kv", None),
        P("req", "kv", None),
        P(None, "req", None),
        P("req"),
    )
    return jax.shard_map(body, mesh=mesh, in_specs=in_specs, out_specs=P(None, "req", "kv"), check_vma=False)
```

```python
import functools
import math

import jax
import jax.numpy as jnp
from jax import lax
from jax.experimental import pallas as pl
from jax.experimental.pallas import tpu as pltpu
from jax.sharding import PartitionSpec as P

MESH = pl.DeviceIdType.MESH
F32 = jnp.float32
BF16 = jnp.bfloat16

SIDE = 4
HOLD = 2
STEPS = 2
ROWS = HOLD * STEPS
LAT = 512
ROPE = 64
WIDE = LAT + ROPE
WIDE_PAD = 640
NEVER = -1e30
SENT = 18

RING = [(dy, dx) for dy in range(SIDE) for dx in range(SIDE) if dy or dx]
RING.sort(key=lambda d: -(min(d[0], SIDE - d[0]) + min(d[1], SIDE - d[1])))
LINE = (3, 2, 1)


def split(value):
    high = value.astype(BF16).astype(F32)
    return high, (value - high).astype(BF16).astype(F32)


def with_stats(peak, total, rows):
    lane = lax.broadcasted_iota(jnp.int32, (rows, 128), 1)
    row = lax.broadcasted_iota(jnp.int32, (rows, 128), 0) % ROWS
    result = jnp.zeros((rows, 128), F32)
    for at, part in enumerate((*split(peak), *split(total))):
        result = jnp.where(lane == row + at * ROWS, part, result)
    return result


def kernel(
    q_nope, q_rope, uk, uv, out_w, cache, new_rows, context, out,
    qn_v, qr_v, uk_v, uv_v, w_v, new_v, ctx_v, qx, zq, q_all, keys, latents, scores, vals, stats, ob, rb, spread, ts, tr,
    load_sem, send_sem, recv_sem,
):
    me = lax.axis_index("kv")
    y, z, x = me // 16, (me // 4) % 4, me % 4
    plane = y * 4 + x
    in_plane = [((y + dy) % 4, (x + dx) % 4) for dy, dx in RING]
    in_line = [(z + dz) % 4 for dz in LINE]

    def plane_id(peer):
        return {"kv": peer[0] * 16 + z * 4 + peer[1]}

    def line_id(peer):
        return {"kv": y * 16 + peer * 4 + x}

    loads = [
        pltpu.make_async_copy(src, dst, load_sem.at[k])
        for k, (src, dst) in enumerate(
            [(q_nope, qn_v), (q_rope, qr_v), (uk, uk_v), (context, ctx_v), (new_rows, new_v), (cache.at[0], keys.at[pl.ds(0, WIDE)]), (uv, uv_v), (out_w, w_v)]
        )
    ]
    barrier = pltpu.get_barrier_semaphore()
    for peer in in_plane[:5]:
        pl.semaphore_signal(barrier, inc=1, device_id=plane_id(peer), device_id_type=MESH)
    for peer in in_line:
        pl.semaphore_signal(barrier, inc=1, device_id=line_id(peer), device_id_type=MESH)
    for peer in in_plane[5:]:
        pl.semaphore_signal(barrier, inc=1, device_id=plane_id(peer), device_id_type=MESH)
    for load in loads[:3]:
        load.start()
    for load in loads[3:]:
        load.start()
    l_qn, l_qr, l_uk, l_ctx, l_new, l_cache, l_uv, l_w = loads

    l_qn.wait()
    l_qr.wait()
    l_uk.wait()
    qx[...] = jnp.zeros((8, 128), F32)
    for step in range(STEPS):
        qx[step * 2 : step * 2 + 2, :] = qn_v[step, 0].astype(F32)
    lhs = qx[...].astype(BF16)
    even = lax.broadcasted_iota(jnp.int32, (8, 1), 0) % 2 == 0
    lat = jnp.where(
        even,
        jnp.dot(lhs, uk_v[0], preferred_element_type=F32),
        jnp.dot(lhs, uk_v[1], preferred_element_type=F32),
    )
    zq[z, 0:4, 0:LAT] = lat[0:4].astype(BF16).astype(F32)
    lane = lax.broadcasted_iota(jnp.int32, (2, ROPE), 1)
    for step in range(STEPS):
        flag = jnp.where(lane == step, 1.0, 0.0).astype(F32)
        zq[z, step * 2 : step * 2 + 2, LAT:] = jnp.concatenate(
            [qr_v[step, 0].astype(F32), flag], axis=1
        )

    pl.semaphore_wait(barrier, len(in_plane) + len(in_line))

    def remote(src, dst, phase, device):
        copy = pltpu.make_async_remote_copy(
            src_ref=src,
            dst_ref=dst,
            send_sem=send_sem.at[phase],
            recv_sem=recv_sem.at[phase],
            device_id=device,
            device_id_type=MESH,
        )
        copy.start()

    def take(ref, sem):
        pltpu.make_async_copy(ref, ref, sem).wait()

    mine = zq.at[z, pl.ds(0, 4)]
    for peer in in_line:
        remote(mine, mine, 0, line_id(peer))

    l_ctx.wait()
    l_new.wait()
    l_cache.wait()
    length = ctx_v[...]
    rows = jnp.concatenate([new_v[0].astype(F32), jnp.zeros((STEPS, WIDE_PAD - WIDE), F32)], axis=1)
    appended = jnp.concatenate([rows, jnp.zeros((8 - STEPS, WIDE_PAD), F32)], axis=0).T
    row = lax.broadcasted_iota(jnp.int32, (WIDE_PAD - WIDE, 1), 0)

    def prepare(k, _):
        here = pl.ds(pl.multiple_of(k * 256, 256), 256)
        token = (lax.broadcasted_iota(jnp.int32, (1, 256), 1) + k * 256) * 64 + me
        block = keys[0:WIDE, here].astype(F32)
        for step in range(STEPS):
            block = jnp.where(token == length + step, appended[0:WIDE, step : step + 1], block)
        keys[0:WIDE, here] = block.astype(BF16)
        latents[here, :] = block[0:LAT].astype(BF16).T
        mask = jnp.where((row < STEPS) & (token > length + row), NEVER, 0.0)
        keys[WIDE:, here] = mask.astype(BF16)
        return 0

    lax.fori_loop(0, 4, prepare, 0)

    take(zq.at[pl.ds(0, 3), pl.ds(0, 4)], recv_sem.at[0])
    mine = q_all.at[pl.ds(pl.multiple_of(plane * 16, 16), 16)]
    mine[...] = jnp.concatenate([zq[k, 0:4, :] for k in range(4)], axis=0).astype(BF16)
    for peer in in_plane:
        remote(mine, mine, 1, plane_id(peer))
    lax.fori_loop(4, 8, prepare, 0)
    column = lax.broadcasted_iota(jnp.int32, (128, 1024), 1) // 16
    place = lax.broadcasted_iota(jnp.int32, (128, 1024), 0)
    spread[...] = jnp.where(column == place, 1.0, 0.0).astype(BF16)
    take(q_all.at[pl.ds(0, 240)], recv_sem.at[1])

    scale = math.log2(math.e) * (128 + ROPE) ** -0.5

    def attend(part):
        blocks = [pl.ds(pl.multiple_of(to_y * 64, 64), 64) for to_y in part]
        queries = jnp.concatenate([q_all[block, :] for block in blocks], axis=0)
        peak = None
        for k in range(4):
            tiles = jnp.dot(queries, keys[:, k * 512 : k * 512 + 512], preferred_element_type=F32)
            scores[:, k * 512 : k * 512 + 512] = tiles
            for j in range(4):
                tile = tiles[:, j * 128 : j * 128 + 128]
                peak = tile if peak is None else jnp.maximum(peak, tile)
        high, low = split(jnp.max(peak, axis=1, keepdims=True) * scale)
        peak = high + low
        total = jnp.zeros((128, 128), F32)
        value = jnp.zeros((128, LAT), F32)
        for k in range(4):
            expo = jnp.exp2(scores[:, k * 512 : k * 512 + 512] * scale - peak)
            for j in range(4):
                total = total + expo[:, j * 128 : j * 128 + 128]
            value = value + jnp.dot(
                expo.astype(BF16), latents[k * 512 : k * 512 + 512, :], preferred_element_type=F32
            )
        note = with_stats(peak, jnp.sum(total, axis=1, keepdims=True), 128)
        for k, block in enumerate(blocks):
            vals[block, :] = value[k * 64 : k * 64 + 64]
            stats[block, :] = note[k * 64 : k * 64 + 64]

    low_half = lax.broadcasted_iota(jnp.int32, (8, 1), 0) < 4

    def halves(left, right):
        return (
            jnp.where(low_half, left, pltpu.roll(right, 4, 0)),
            jnp.where(low_half, pltpu.roll(left, 4, 0), right),
        )

    own_pair = z // 2

    def deliver(part, z_pair, last=False):
        for dy, to_y in enumerate(part):
            for dx in (2, 1, 3, 0):
                to_x = (x + dx) % 4
                eight = pl.ds(pl.multiple_of(((to_y * 4 + to_x) * 2 + z_pair) * 8, 8), 8)
                quarters = [vals[eight, k * 128 : k * 128 + 128] for k in range(4)]
                first, second = zip(halves(*quarters[:2]), halves(*quarters[2:]))
                note = stats[eight, :]
                note = note + pltpu.roll(note, 1, 0)
                note = note + pltpu.roll(note, 2, 0)
                for j, (rows, shift) in enumerate(((first, 5), (second, 1))):
                    peer = to_y * 16 + (z_pair * 2 + j) * 4 + to_x
                    ob[peer, 0:16, :] = jnp.concatenate(rows, axis=0).astype(BF16)
                    moved = pltpu.roll(note, shift, 0)
                    ob[peer, 16:32, :] = jnp.concatenate([moved, moved], axis=0).astype(BF16)
                for j in (1, 0):
                    peer = to_y * 16 + (z_pair * 2 + (z + j) % 2) * 4 + to_x
                    if last and dy == 1 and dx == 0 and j == 0:
                        rb[me] = ob[me]
                    else:
                        remote(ob.at[peer, pl.ds(0, SENT)], rb.at[me, pl.ds(0, SENT)], 2, {"kv": peer})

    far = ((y + 2) % 4, (y + 3) % 4)
    near = ((y + 1) % 4, y)
    attend(far)
    deliver(far, 1 - own_pair)
    attend(near)
    deliver(near, 1 - own_pair)
    deliver(far, own_pair)
    deliver(near, own_pair, last=True)
    l_uv.wait()
    l_w.wait()
    take(rb.at[pl.ds(0, 63), pl.ds(0, SENT)], recv_sem.at[2])
    notes = jnp.concatenate(
        [rb[k, 16:18, :].astype(F32)[0:1] for k in range(64)] + [jnp.zeros((64, 128), F32)], axis=0
    ).T
    known = lax.broadcasted_iota(jnp.int32, (ROWS, 128), 1) < 64
    peak = jnp.where(known, notes[0:4] + notes[4:8], -3e38)
    factor = jnp.where(known, jnp.exp2(peak - jnp.max(peak, axis=1, keepdims=True)), 0.0)
    whole = jnp.sum(factor * (notes[8:12] + notes[12:16]), axis=1, keepdims=True)
    factor = factor / whole
    factor = jnp.concatenate([factor, factor], axis=0).astype(BF16)
    factor = jnp.dot(factor, spread[...], preferred_element_type=F32)
    column = lax.broadcasted_iota(jnp.int32, (16, 1024), 1) % 16
    place = lax.broadcasted_iota(jnp.int32, (16, 1024), 0)
    factor = jnp.where(column == place, jnp.concatenate([factor, factor], axis=0), 0.0).astype(BF16)
    joined = jnp.dot(
        factor, rb[:, 0:16, :].reshape(1024, 128), preferred_element_type=F32
    )
    top, bottom = joined[0:8], joined[8:16]
    latent = jnp.concatenate(
        [top, pltpu.roll(top, 4, 0), bottom, pltpu.roll(bottom, 4, 0)], axis=1
    ).astype(BF16)

    head_value = jnp.concatenate(
        [
            jnp.where(even, jnp.dot(latent, uv_v[0], preferred_element_type=F32), 0.0),
            jnp.where(even, 0.0, jnp.dot(latent, uv_v[1], preferred_element_type=F32)),
        ],
        axis=1,
    )
    pairs = head_value + pltpu.roll(head_value, 7, 0)
    first = lax.broadcasted_iota(jnp.int32, (8, 1), 0) == 0
    flat = jnp.where(first, pairs, pltpu.roll(pairs, 7, 0)).astype(BF16)
    for z_pair in (1 - own_pair, own_pair):
        for dy in (2, 1, 3, 0):
            group = ((y + dy) % 4) * 2 + z_pair
            columns = pl.ds(pl.multiple_of(group * 896, 128), 896)
            term = jnp.dot(flat, w_v[:, columns], preferred_element_type=F32)
            for j in range(8):
                ts[group * 8 + j, :, 0:112] = term[:, j * 112 : j * 112 + 112]
            for dx in (2, 1, 3, 0):
                for dz in (1, 0):
                    peer = group * 8 + ((z + dz) % 2) * 4 + (x + dx) % 4
                    if z_pair is own_pair and dy == 0 and dx == 0 and dz == 0:
                        tr[me, 0:2, :] = ts[me, 0:2, :]
                    else:
                        remote(ts.at[peer, pl.ds(0, 2)], tr.at[me, pl.ds(0, 2)], 3, {"kv": peer})
    take(tr.at[pl.ds(0, 63), pl.ds(0, 2)], recv_sem.at[3])
    result = jnp.sum(tr[:, 0:2, :], axis=0)
    out[0] = result[:, 0:112].astype(BF16)

    take(zq.at[pl.ds(0, 3), pl.ds(0, 4)], send_sem.at[0])
    take(q_all.at[pl.ds(0, 240)], send_sem.at[1])
    take(ob.at[pl.ds(0, 63), pl.ds(0, SENT)], send_sem.at[2])
    take(ts.at[pl.ds(0, 63), pl.ds(0, 2)], send_sem.at[3])


def body(q_nope, q_rope, uk, uv, out_w, cache, new_rows, context):
    hbm = pl.BlockSpec(memory_space=pltpu.HBM)
    result = pl.pallas_call(
        kernel,
        out_shape=pltpu.VMEM((1, STEPS, 112), BF16),
        in_specs=[hbm] * 8,
        out_specs=pl.BlockSpec(memory_space=pltpu.VMEM),
        scratch_shapes=[
            pltpu.VMEM((2, 1, 2, 128), BF16),
            pltpu.VMEM((2, 1, 2, ROPE), BF16),
            pltpu.VMEM((2, 128, LAT), BF16),
            pltpu.VMEM((2, LAT, 128), BF16),
            pltpu.VMEM((256, 7168), BF16),
            pltpu.VMEM((1, 2, WIDE), BF16),
            pltpu.VMEM((1, 1), jnp.int32),
            pltpu.VMEM((8, 128), F32),
            pltpu.VMEM((4, 8, WIDE_PAD), F32),
            pltpu.VMEM((256, WIDE_PAD), BF16),
            pltpu.VMEM((WIDE_PAD, 2048), BF16),
            pltpu.VMEM((2048, LAT), BF16),
            pltpu.VMEM((128, 2048), F32),
            pltpu.VMEM((256, LAT), F32),
            pltpu.VMEM((256, 128), F32),
            pltpu.VMEM((64, 32, 128), BF16),
            pltpu.VMEM((64, 32, 128), BF16),
            pltpu.VMEM((128, 1024), BF16),
            pltpu.VMEM((64, 8, 128), F32),
            pltpu.VMEM((64, 8, 128), F32),
            pltpu.SemaphoreType.DMA((8,)),
            pltpu.SemaphoreType.DMA((4,)),
            pltpu.SemaphoreType.DMA((4,)),
        ],
        compiler_params=pltpu.CompilerParams(
            collective_id=0, has_side_effects=True, vmem_limit_bytes=60 << 20
        ),
    )(q_nope, q_rope, uk, uv, out_w, jnp.swapaxes(cache, 1, 2), jnp.swapaxes(new_rows, 0, 1), context.reshape(1, 1))
    return jnp.swapaxes(result, 0, 1)


def solution(mesh):
    in_specs = (
        P(None, "req", "kv", None),
        P(None, "req", "kv", None),
        P("kv", None, None),
        P("kv", None, None),
        P("kv", None),
        P("req", "kv", None),
        P(None, "req", None),
        P("req"),
    )
    return jax.shard_map(body, mesh=mesh, in_specs=in_specs, out_specs=P(None, "req", "kv"), check_vma=False)
```

```python
import functools
import math

import jax
import jax.numpy as jnp
from jax import lax
from jax.experimental import pallas as pl
from jax.experimental.pallas import tpu as pltpu
from jax.sharding import PartitionSpec as P

MESH = pl.DeviceIdType.MESH
F32 = jnp.float32
BF16 = jnp.bfloat16

SIDE = 4
HOLD = 2
STEPS = 2
ROWS = HOLD * STEPS
LAT = 512
ROPE = 64
WIDE = LAT + ROPE
WIDE_PAD = 640
NEVER = -1e30
ASKED = 20
SENT = 18

RING = [(dy, dx) for dy in range(SIDE) for dx in range(SIDE) if dy or dx]
RING.sort(key=lambda d: -(min(d[0], SIDE - d[0]) + min(d[1], SIDE - d[1])))


def split(value):
    high = value.astype(BF16).astype(F32)
    return high, (value - high).astype(BF16).astype(F32)


def with_stats(peak, total, rows):
    lane = lax.broadcasted_iota(jnp.int32, (rows, 128), 1)
    row = lax.broadcasted_iota(jnp.int32, (rows, 128), 0) % ROWS
    result = jnp.zeros((rows, 128), F32)
    for at, part in enumerate((*split(peak), *split(total))):
        result = jnp.where(lane == row + at * ROWS, part, result)
    return result


def kernel(
    q_nope, q_rope, uk, uv, out_w, cache, new_rows, context, out,
    qn_v, qr_v, uk_v, uv_v, w_v, new_v, ctx_v, qx, qs, q_all, keys, latents, scores, vals, stats, ob, rb, spread, ts, tr,
    load_sem, send_sem, recv_sem,
):
    me = lax.axis_index("kv")
    y, z, x = me // 16, (me // 4) % 4, me % 4
    in_plane = [((y + dy) % 4, (x + dx) % 4) for dy, dx in RING]
    own_pair = z // 2
    in_line = [3 - 3 * own_pair, 2 - own_pair, z + 1 - 2 * (z % 2)]

    def plane_id(peer):
        return {"kv": peer[0] * 16 + z * 4 + peer[1]}

    def line_id(peer):
        return {"kv": y * 16 + peer * 4 + x}

    loads = [
        pltpu.make_async_copy(src, dst, load_sem.at[k])
        for k, (src, dst) in enumerate(
            [(q_nope, qn_v), (q_rope, qr_v), (uk, uk_v), (context, ctx_v), (new_rows, new_v), (cache.at[0], keys.at[pl.ds(0, WIDE)]), (uv, uv_v), (out_w, w_v)]
        )
    ]
    barrier = pltpu.get_barrier_semaphore()
    for peer in in_plane[:5]:
        pl.semaphore_signal(barrier, inc=1, device_id=plane_id(peer), device_id_type=MESH)
    for peer in in_line:
        pl.semaphore_signal(barrier, inc=1, device_id=line_id(peer), device_id_type=MESH)
    for peer in in_plane[5:]:
        pl.semaphore_signal(barrier, inc=1, device_id=plane_id(peer), device_id_type=MESH)
    for load in loads[:3]:
        load.start()
    for load in loads[3:]:
        load.start()
    l_qn, l_qr, l_uk, l_ctx, l_new, l_cache, l_uv, l_w = loads

    l_qn.wait()
    l_qr.wait()
    l_uk.wait()
    low_half = lax.broadcasted_iota(jnp.int32, (8, 1), 0) < 4

    def halves(left, right):
        return (
            jnp.where(low_half, left, pltpu.roll(right, 4, 0)),
            jnp.where(low_half, pltpu.roll(left, 4, 0), right),
        )

    qx[...] = jnp.zeros((8, 128), F32)
    for step in range(STEPS):
        qx[step * 2 : step * 2 + 2, :] = qn_v[step, 0].astype(F32)
    lhs = qx[...].astype(BF16)
    even = lax.broadcasted_iota(jnp.int32, (8, 1), 0) % 2 == 0
    lat = jnp.where(
        even,
        jnp.dot(lhs, uk_v[0], preferred_element_type=F32),
        jnp.dot(lhs, uk_v[1], preferred_element_type=F32),
    )
    quarters = [lat[:, k * 128 : k * 128 + 128] for k in range(4)]
    qs[me, 0:16, :] = jnp.concatenate(
        [halves(*quarters[:2])[0], halves(*quarters[2:])[0]], axis=0
    ).astype(BF16)
    lane = lax.broadcasted_iota(jnp.int32, (2, ROPE), 1)
    for step in range(STEPS):
        flag = jnp.where(lane == step, 1.0, 0.0).astype(F32)
        qx[step * 2 : step * 2 + 2, :] = jnp.concatenate([qr_v[step, 0].astype(F32), flag], axis=1)
    tail = qx[...]
    qs[me, 16:32, :] = jnp.concatenate([tail, tail], axis=0).astype(BF16)

    pl.semaphore_wait(barrier, len(in_plane) + len(in_line))

    def remote(src, dst, sent, arrived, device):
        copy = pltpu.make_async_remote_copy(
            src_ref=src,
            dst_ref=dst,
            send_sem=send_sem.at[sent],
            recv_sem=recv_sem.at[arrived],
            device_id=device,
            device_id_type=MESH,
        )
        copy.start()

    def take(ref, sem):
        pltpu.make_async_copy(ref, ref, sem).wait()

    def slab(owner_z):
        return qs.at[y * 16 + owner_z * 4 + x, pl.ds(0, ASKED)]

    for peer in in_line:
        remote(slab(z), slab(z), 0, z, line_id(peer))
    for peer in in_plane:
        remote(slab(z), slab(z), 1, 4, plane_id(peer))

    l_ctx.wait()
    l_new.wait()
    l_cache.wait()
    length = ctx_v[...]
    rows = jnp.concatenate([new_v[0].astype(F32), jnp.zeros((STEPS, WIDE_PAD - WIDE), F32)], axis=1)
    appended = jnp.concatenate([rows, jnp.zeros((8 - STEPS, WIDE_PAD), F32)], axis=0).T
    row = lax.broadcasted_iota(jnp.int32, (WIDE_PAD - WIDE, 1), 0)

    def prepare(k, _):
        here = pl.ds(pl.multiple_of(k * 256, 256), 256)
        token = (lax.broadcasted_iota(jnp.int32, (1, 256), 1) + k * 256) * 64 + me
        block = keys[0:WIDE, here].astype(F32)
        for step in range(STEPS):
            block = jnp.where(token == length + step, appended[0:WIDE, step : step + 1], block)
        keys[0:WIDE, here] = block.astype(BF16)
        latents[here, :] = block[0:LAT].astype(BF16).T
        mask = jnp.where((row < STEPS) & (token > length + row), NEVER, 0.0)
        keys[WIDE:, here] = mask.astype(BF16)
        return 0

    def unpack(z_pair):
        for to_y in range(4):
            for to_x in range(4):
                owner = to_y * 16 + z_pair * 8 + to_x
                parts = [[qs[owner + j, k * 8 : k * 8 + 8, :].astype(F32) for k in range(3)] for j in (0, 4)]
                eight = pl.ds(pl.multiple_of((to_y * 4 + to_x) * 16 + z_pair * 8, 8), 8)
                for k in range(3):
                    pieces = halves(parts[0][k], parts[1][k])
                    q_all[eight, k * 256 : k * 256 + 128] = pieces[0]
                    if k < 2:
                        q_all[eight, k * 256 + 128 : k * 256 + 256] = pieces[1]

    done = 0
    for k, chunks in ((2, 2), (1, 1), (0, 1)):
        lax.fori_loop(done, done + chunks, prepare, 0)
        done += chunks
        take(slab(in_line[k]), recv_sem.at[in_line[k]])
        for peer in in_plane:
            remote(slab(in_line[k]), slab(in_line[k]), 1, 7 - k, plane_id(peer))
    lax.fori_loop(done, 8, prepare, 0)
    column = lax.broadcasted_iota(jnp.int32, (128, 1024), 1) // 16
    place = lax.broadcasted_iota(jnp.int32, (128, 1024), 0)
    spread[...] = jnp.where(column == place, 1.0, 0.0).astype(BF16)
    for k in range(4):
        take(qs.at[pl.ds(0, 15), pl.ds(0, ASKED)], recv_sem.at[4 + k])
        if k == 1:
            unpack(own_pair)
    unpack(1 - own_pair)

    scale = math.log2(math.e) * (128 + ROPE) ** -0.5

    def attend(part):
        blocks = [pl.ds(pl.multiple_of(to_y * 64, 64), 64) for to_y in part]
        queries = jnp.concatenate([q_all[block, :] for block in blocks], axis=0).astype(BF16)
        peak = None
        for k in range(4):
            tiles = jnp.dot(queries, keys[:, k * 512 : k * 512 + 512], preferred_element_type=F32)
            scores[:, k * 512 : k * 512 + 512] = tiles
            for j in range(4):
                tile = tiles[:, j * 128 : j * 128 + 128]
                peak = tile if peak is None else jnp.maximum(peak, tile)
        high, low = split(jnp.max(peak, axis=1, keepdims=True) * scale)
        peak = high + low
        total = jnp.zeros((128, 128), F32)
        value = jnp.zeros((128, LAT), F32)
        for k in range(4):
            expo = jnp.exp2(scores[:, k * 512 : k * 512 + 512] * scale - peak)
            for j in range(4):
                total = total + expo[:, j * 128 : j * 128 + 128]
            value = value + jnp.dot(
                expo.astype(BF16), latents[k * 512 : k * 512 + 512, :], preferred_element_type=F32
            )
        note = with_stats(peak, jnp.sum(total, axis=1, keepdims=True), 128)
        for k, block in enumerate(blocks):
            vals[block, :] = value[k * 64 : k * 64 + 64]
            stats[block, :] = note[k * 64 : k * 64 + 64]

    def deliver(part, z_pair, last=False):
        for dy, to_y in enumerate(part):
            for dx in (2, 1, 3, 0):
                to_x = (x + dx) % 4
                eight = pl.ds(pl.multiple_of(((to_y * 4 + to_x) * 2 + z_pair) * 8, 8), 8)
                quarters = [vals[eight, k * 128 : k * 128 + 128] for k in range(4)]
                first, second = zip(halves(*quarters[:2]), halves(*quarters[2:]))
                note = stats[eight, :]
                note = note + pltpu.roll(note, 1, 0)
                note = note + pltpu.roll(note, 2, 0)
                for j, (rows, shift) in enumerate(((first, 5), (second, 1))):
                    peer = to_y * 16 + (z_pair * 2 + j) * 4 + to_x
                    ob[peer, 0:16, :] = jnp.concatenate(rows, axis=0).astype(BF16)
                    moved = pltpu.roll(note, shift, 0)
                    ob[peer, 16:32, :] = jnp.concatenate([moved, moved], axis=0).astype(BF16)
                for j in (1, 0):
                    peer = to_y * 16 + (z_pair * 2 + (z + j) % 2) * 4 + to_x
                    if last and dy == 1 and dx == 0 and j == 0:
                        rb[me] = ob[me]
                    else:
                        remote(ob.at[peer, pl.ds(0, SENT)], rb.at[me, pl.ds(0, SENT)], 2, 8, {"kv": peer})

    far = ((y + 2) % 4, (y + 3) % 4)
    near = ((y + 1) % 4, y)
    attend(far)
    deliver(far, 1 - own_pair)
    attend(near)
    deliver(near, 1 - own_pair)
    deliver(far, own_pair)
    deliver(near, own_pair, last=True)
    l_uv.wait()
    l_w.wait()
    take(rb.at[pl.ds(0, 63), pl.ds(0, SENT)], recv_sem.at[8])
    notes = jnp.concatenate(
        [rb[k, 16:18, :].astype(F32)[0:1] for k in range(64)] + [jnp.zeros((64, 128), F32)], axis=0
    ).T
    known = lax.broadcasted_iota(jnp.int32, (ROWS, 128), 1) < 64
    peak = jnp.where(known, notes[0:4] + notes[4:8], -3e38)
    factor = jnp.where(known, jnp.exp2(peak - jnp.max(peak, axis=1, keepdims=True)), 0.0)
    whole = jnp.sum(factor * (notes[8:12] + notes[12:16]), axis=1, keepdims=True)
    factor = factor / whole
    factor = jnp.concatenate([factor, factor], axis=0).astype(BF16)
    factor = jnp.dot(factor, spread[...], preferred_element_type=F32)
    column = lax.broadcasted_iota(jnp.int32, (16, 1024), 1) % 16
    place = lax.broadcasted_iota(jnp.int32, (16, 1024), 0)
    factor = jnp.where(column == place, jnp.concatenate([factor, factor], axis=0), 0.0).astype(BF16)
    joined = jnp.dot(
        factor, rb[:, 0:16, :].reshape(1024, 128), preferred_element_type=F32
    )
    top, bottom = joined[0:8], joined[8:16]
    latent = jnp.concatenate(
        [top, pltpu.roll(top, 4, 0), bottom, pltpu.roll(bottom, 4, 0)], axis=1
    ).astype(BF16)

    head_value = jnp.concatenate(
        [
            jnp.where(even, jnp.dot(latent, uv_v[0], preferred_element_type=F32), 0.0),
            jnp.where(even, 0.0, jnp.dot(latent, uv_v[1], preferred_element_type=F32)),
        ],
        axis=1,
    )
    pairs = head_value + pltpu.roll(head_value, 7, 0)
    first = lax.broadcasted_iota(jnp.int32, (8, 1), 0) == 0
    flat = jnp.where(first, pairs, pltpu.roll(pairs, 7, 0)).astype(BF16)
    for z_pair in (1 - own_pair, own_pair):
        for dy in (2, 1, 3, 0):
            group = ((y + dy) % 4) * 2 + z_pair
            columns = pl.ds(pl.multiple_of(group * 896, 128), 896)
            term = jnp.dot(flat, w_v[:, columns], preferred_element_type=F32)
            for j in range(8):
                ts[group * 8 + j, :, 0:112] = term[:, j * 112 : j * 112 + 112]
            for dx in (2, 1, 3, 0):
                for dz in (1, 0):
                    peer = group * 8 + ((z + dz) % 2) * 4 + (x + dx) % 4
                    if z_pair is own_pair and dy == 0 and dx == 0 and dz == 0:
                        tr[me, 0:2, :] = ts[me, 0:2, :]
                    else:
                        remote(ts.at[peer, pl.ds(0, 2)], tr.at[me, pl.ds(0, 2)], 3, 9, {"kv": peer})
    take(tr.at[pl.ds(0, 63), pl.ds(0, 2)], recv_sem.at[9])
    result = jnp.sum(tr[:, 0:2, :], axis=0)
    out[0] = result[:, 0:112].astype(BF16)

    take(qs.at[pl.ds(0, 3), pl.ds(0, ASKED)], send_sem.at[0])
    take(qs.at[pl.ds(0, 60), pl.ds(0, ASKED)], send_sem.at[1])
    take(ob.at[pl.ds(0, 63), pl.ds(0, SENT)], send_sem.at[2])
    take(ts.at[pl.ds(0, 63), pl.ds(0, 2)], send_sem.at[3])


def body(q_nope, q_rope, uk, uv, out_w, cache, new_rows, context):
    hbm = pl.BlockSpec(memory_space=pltpu.HBM)
    result = pl.pallas_call(
        kernel,
        out_shape=pltpu.VMEM((1, STEPS, 112), BF16),
        in_specs=[hbm] * 8,
        out_specs=pl.BlockSpec(memory_space=pltpu.VMEM),
        scratch_shapes=[
            pltpu.VMEM((2, 1, 2, 128), BF16),
            pltpu.VMEM((2, 1, 2, ROPE), BF16),
            pltpu.VMEM((2, 128, LAT), BF16),
            pltpu.VMEM((2, LAT, 128), BF16),
            pltpu.VMEM((256, 7168), BF16),
            pltpu.VMEM((1, 2, WIDE), BF16),
            pltpu.VMEM((1, 1), jnp.int32),
            pltpu.VMEM((8, 128), F32),
            pltpu.VMEM((64, 32, 128), BF16),
            pltpu.VMEM((256, WIDE_PAD), F32),
            pltpu.VMEM((WIDE_PAD, 2048), BF16),
            pltpu.VMEM((2048, LAT), BF16),
            pltpu.VMEM((128, 2048), F32),
            pltpu.VMEM((256, LAT), F32),
            pltpu.VMEM((256, 128), F32),
            pltpu.VMEM((64, 32, 128), BF16),
            pltpu.VMEM((64, 32, 128), BF16),
            pltpu.VMEM((128, 1024), BF16),
            pltpu.VMEM((64, 8, 128), F32),
            pltpu.VMEM((64, 8, 128), F32),
            pltpu.SemaphoreType.DMA((8,)),
            pltpu.SemaphoreType.DMA((4,)),
            pltpu.SemaphoreType.DMA((10,)),
        ],
        compiler_params=pltpu.CompilerParams(
            collective_id=0, has_side_effects=True, vmem_limit_bytes=60 << 20
        ),
    )(q_nope, q_rope, uk, uv, out_w, jnp.swapaxes(cache, 1, 2), jnp.swapaxes(new_rows, 0, 1), context.reshape(1, 1))
    return jnp.swapaxes(result, 0, 1)


def solution(mesh):
    in_specs = (
        P(None, "req", "kv", None),
        P(None, "req", "kv", None),
        P("kv", None, None),
        P("kv", None, None),
        P("kv", None),
        P("req", "kv", None),
        P(None, "req", None),
        P("req"),
    )
    return jax.shard_map(body, mesh=mesh, in_specs=in_specs, out_specs=P(None, "req", "kv"), check_vma=False)
```

```python
import functools
import math

import jax
import jax.numpy as jnp
from jax import lax
from jax.experimental import pallas as pl
from jax.experimental.pallas import tpu as pltpu
from jax.sharding import PartitionSpec as P

MESH = pl.DeviceIdType.MESH
F32 = jnp.float32
BF16 = jnp.bfloat16

SIDE = 4
HOLD = 2
STEPS = 2
ROWS = HOLD * STEPS
LAT = 512
ROPE = 64
WIDE = LAT + ROPE
WIDE_PAD = 640
NEVER = -1e30
ASKED = 20
SENT = 18

RING = [(dy, dx) for dy in range(SIDE) for dx in range(SIDE) if dy or dx]
RING.sort(key=lambda d: -(min(d[0], SIDE - d[0]) + min(d[1], SIDE - d[1])))


def split(value):
    high = value.astype(BF16).astype(F32)
    return high, (value - high).astype(BF16).astype(F32)


def with_stats(peak, total, rows):
    lane = lax.broadcasted_iota(jnp.int32, (rows, 128), 1)
    row = lax.broadcasted_iota(jnp.int32, (rows, 128), 0) % ROWS
    result = jnp.zeros((rows, 128), F32)
    for at, part in enumerate((*split(peak), *split(total))):
        result = jnp.where(lane == row + at * ROWS, part, result)
    return result


def kernel(
    q_nope, q_rope, uk, uv, out_w, cache, new_rows, context, out,
    qn_v, qr_v, uk_v, uv_v, w_v, w_p, new_v, ctx_v, qx, qs, q_all, keys, latents, scores, vals, stats, ob, rb, spread, ts, tr,
    load_sem, send_sem, recv_sem,
):
    me = lax.axis_index("kv")
    y, z, x = me // 16, (me // 4) % 4, me % 4
    in_plane = [((y + dy) % 4, (x + dx) % 4) for dy, dx in RING]
    own_pair = z // 2
    in_line = [3 - 3 * own_pair, 2 - own_pair, z + 1 - 2 * (z % 2)]

    def plane_id(peer):
        return {"kv": peer[0] * 16 + z * 4 + peer[1]}

    def line_id(peer):
        return {"kv": y * 16 + peer * 4 + x}

    loads = [
        pltpu.make_async_copy(src, dst, load_sem.at[k])
        for k, (src, dst) in enumerate(
            [(q_nope, qn_v), (q_rope, qr_v), (uk, uk_v), (context, ctx_v), (new_rows, new_v), (cache.at[0], keys.at[pl.ds(0, WIDE)]), (uv, uv_v), (out_w, w_v)]
        )
    ]
    barrier = pltpu.get_barrier_semaphore()
    for peer in in_plane[:5]:
        pl.semaphore_signal(barrier, inc=1, device_id=plane_id(peer), device_id_type=MESH)
    for peer in in_line:
        pl.semaphore_signal(barrier, inc=1, device_id=line_id(peer), device_id_type=MESH)
    for peer in in_plane[5:]:
        pl.semaphore_signal(barrier, inc=1, device_id=plane_id(peer), device_id_type=MESH)
    for load in loads[:3]:
        load.start()
    for load in loads[3:]:
        load.start()
    l_qn, l_qr, l_uk, l_ctx, l_new, l_cache, l_uv, l_w = loads

    l_qn.wait()
    l_qr.wait()
    l_uk.wait()
    low_half = lax.broadcasted_iota(jnp.int32, (8, 1), 0) < 4

    def halves(left, right):
        return (
            jnp.where(low_half, left, pltpu.roll(right, 4, 0)),
            jnp.where(low_half, pltpu.roll(left, 4, 0), right),
        )

    qx[...] = jnp.zeros((8, 128), F32)
    for step in range(STEPS):
        qx[step * 2 : step * 2 + 2, :] = qn_v[step, 0].astype(F32)
    lhs = qx[...].astype(BF16)
    even = lax.broadcasted_iota(jnp.int32, (8, 1), 0) % 2 == 0
    lat = jnp.where(
        even,
        jnp.dot(lhs, uk_v[0], preferred_element_type=F32),
        jnp.dot(lhs, uk_v[1], preferred_element_type=F32),
    )
    quarters = [lat[:, k * 128 : k * 128 + 128] for k in range(4)]
    qs[me, 0:16, :] = jnp.concatenate(
        [halves(*quarters[:2])[0], halves(*quarters[2:])[0]], axis=0
    ).astype(BF16)
    lane = lax.broadcasted_iota(jnp.int32, (2, ROPE), 1)
    for step in range(STEPS):
        flag = jnp.where(lane == step, 1.0, 0.0).astype(F32)
        qx[step * 2 : step * 2 + 2, :] = jnp.concatenate([qr_v[step, 0].astype(F32), flag], axis=1)
    tail = qx[...]
    qs[me, 16:32, :] = jnp.concatenate([tail, tail], axis=0).astype(BF16)

    pl.semaphore_wait(barrier, len(in_plane) + len(in_line))

    def remote(src, dst, sent, arrived, device):
        copy = pltpu.make_async_remote_copy(
            src_ref=src,
            dst_ref=dst,
            send_sem=send_sem.at[sent],
            recv_sem=recv_sem.at[arrived],
            device_id=device,
            device_id_type=MESH,
        )
        copy.start()

    def take(ref, sem):
        pltpu.make_async_copy(ref, ref, sem).wait()

    def slab(owner_z):
        return qs.at[y * 16 + owner_z * 4 + x, pl.ds(0, ASKED)]

    for peer in in_line:
        remote(slab(z), slab(z), 0, z, line_id(peer))
    for peer in in_plane:
        remote(slab(z), slab(z), 1, 4, plane_id(peer))

    l_ctx.wait()
    l_new.wait()
    l_cache.wait()
    length = ctx_v[...]
    rows = jnp.concatenate([new_v[0].astype(F32), jnp.zeros((STEPS, WIDE_PAD - WIDE), F32)], axis=1)
    appended = jnp.concatenate([rows, jnp.zeros((8 - STEPS, WIDE_PAD), F32)], axis=0).T
    row = lax.broadcasted_iota(jnp.int32, (WIDE_PAD - WIDE, 1), 0)

    def prepare(k, _):
        here = pl.ds(pl.multiple_of(k * 256, 256), 256)
        token = (lax.broadcasted_iota(jnp.int32, (1, 256), 1) + k * 256) * 64 + me
        block = keys[0:WIDE, here].astype(F32)
        for step in range(STEPS):
            block = jnp.where(token == length + step, appended[0:WIDE, step : step + 1], block)
        keys[0:WIDE, here] = block.astype(BF16)
        latents[here, :] = block[0:LAT].astype(BF16).T
        mask = jnp.where((row < STEPS) & (token > length + row), NEVER, 0.0)
        keys[WIDE:, here] = mask.astype(BF16)
        return 0

    def unpack(z_pair):
        for to_y in range(4):
            for to_x in range(4):
                owner = to_y * 16 + z_pair * 8 + to_x
                parts = [[qs[owner + j, k * 8 : k * 8 + 8, :].astype(F32) for k in range(3)] for j in (0, 4)]
                eight = pl.ds(pl.multiple_of(z_pair * 128 + (to_y * 4 + to_x) * 8, 8), 8)
                for k in range(3):
                    pieces = halves(parts[0][k], parts[1][k])
                    q_all[eight, k * 256 : k * 256 + 128] = pieces[0]
                    if k < 2:
                        q_all[eight, k * 256 + 128 : k * 256 + 256] = pieces[1]

    done = 0
    for k, chunks in ((2, 2), (1, 1), (0, 1)):
        lax.fori_loop(done, done + chunks, prepare, 0)
        done += chunks
        take(slab(in_line[k]), recv_sem.at[in_line[k]])
        for peer in in_plane:
            remote(slab(in_line[k]), slab(in_line[k]), 1, 7 - k, plane_id(peer))
    lax.fori_loop(done, 8, prepare, 0)
    column = lax.broadcasted_iota(jnp.int32, (128, 1024), 1) // 16
    place = lax.broadcasted_iota(jnp.int32, (128, 1024), 0)
    spread[...] = jnp.where(column == place, 1.0, 0.0).astype(BF16)

    scale = math.log2(math.e) * (128 + ROPE) ** -0.5

    def attend(z_pair):
        half = pl.ds(pl.multiple_of(z_pair * 128, 128), 128)
        queries = q_all[half, :].astype(BF16)
        peak = None
        for k in range(4):
            tiles = jnp.dot(queries, keys[:, k * 512 : k * 512 + 512], preferred_element_type=F32)
            scores[:, k * 512 : k * 512 + 512] = tiles
            for j in range(4):
                tile = tiles[:, j * 128 : j * 128 + 128]
                peak = tile if peak is None else jnp.maximum(peak, tile)
        high, low = split(jnp.max(peak, axis=1, keepdims=True) * scale)
        peak = high + low
        total = jnp.zeros((128, 128), F32)
        value = jnp.zeros((128, LAT), F32)
        for k in range(4):
            expo = jnp.exp2(scores[:, k * 512 : k * 512 + 512] * scale - peak)
            for j in range(4):
                total = total + expo[:, j * 128 : j * 128 + 128]
            value = value + jnp.dot(
                expo.astype(BF16), latents[k * 512 : k * 512 + 512, :], preferred_element_type=F32
            )
        vals[half, :] = value
        stats[half, :] = with_stats(peak, jnp.sum(total, axis=1, keepdims=True), 128)

    def deliver(z_pair):
        for dy, dx in (*RING, (0, 0)):
            to_y, to_x = (y + dy) % 4, (x + dx) % 4
            eight = pl.ds(pl.multiple_of(z_pair * 128 + (to_y * 4 + to_x) * 8, 8), 8)
            quarters = [vals[eight, k * 128 : k * 128 + 128] for k in range(4)]
            first, second = zip(halves(*quarters[:2]), halves(*quarters[2:]))
            note = stats[eight, :]
            note = note + pltpu.roll(note, 1, 0)
            note = note + pltpu.roll(note, 2, 0)
            for j, (rows, shift) in enumerate(((first, 5), (second, 1))):
                peer = to_y * 16 + (z_pair * 2 + j) * 4 + to_x
                ob[peer, 0:16, :] = jnp.concatenate(rows, axis=0).astype(BF16)
                moved = pltpu.roll(note, shift, 0)
                ob[peer, 16:32, :] = jnp.concatenate([moved, moved], axis=0).astype(BF16)
            for j in (1, 0):
                peer = to_y * 16 + (z_pair * 2 + (z + j) % 2) * 4 + to_x
                if z_pair is own_pair and dy == 0 and dx == 0 and j == 0:
                    rb[me] = ob[me]
                else:
                    remote(ob.at[peer, pl.ds(0, SENT)], rb.at[me, pl.ds(0, SENT)], 2, 8, {"kv": peer})

    def arrived(k):
        take(qs.at[pl.ds(0, 15), pl.ds(0, ASKED)], recv_sem.at[4 + k])

    arrived(0)
    arrived(1)
    unpack(own_pair)
    attend(own_pair)
    arrived(2)
    arrived(3)
    unpack(1 - own_pair)
    attend(1 - own_pair)
    deliver(1 - own_pair)
    deliver(own_pair)
    l_uv.wait()
    l_w.wait()

    def align(group, _):
        columns = w_v[:, pl.ds(pl.multiple_of(group * 896, 128), 896)]
        gap = jnp.zeros((256, 16), BF16)
        w_p[:, pl.ds(pl.multiple_of(group * 1024, 128), 1024)] = jnp.concatenate(
            [piece for j in range(8) for piece in (columns[:, j * 112 : j * 112 + 112], gap)], axis=1
        )
        return 0

    lax.fori_loop(0, 8, align, 0)
    take(rb.at[pl.ds(0, 63), pl.ds(0, SENT)], recv_sem.at[8])
    notes = jnp.concatenate(
        [rb[k, 16:18, :].astype(F32)[0:1] for k in range(64)] + [jnp.zeros((64, 128), F32)], axis=0
    ).T
    known = lax.broadcasted_iota(jnp.int32, (ROWS, 128), 1) < 64
    peak = jnp.where(known, notes[0:4] + notes[4:8], -3e38)
    factor = jnp.where(known, jnp.exp2(peak - jnp.max(peak, axis=1, keepdims=True)), 0.0)
    whole = jnp.sum(factor * (notes[8:12] + notes[12:16]), axis=1, keepdims=True)
    factor = factor / whole
    factor = jnp.concatenate([factor, factor], axis=0).astype(BF16)
    factor = jnp.dot(factor, spread[...], preferred_element_type=F32)
    column = lax.broadcasted_iota(jnp.int32, (16, 1024), 1) % 16
    place = lax.broadcasted_iota(jnp.int32, (16, 1024), 0)
    factor = jnp.where(column == place, jnp.concatenate([factor, factor], axis=0), 0.0).astype(BF16)
    joined = jnp.dot(
        factor, rb[:, 0:16, :].reshape(1024, 128), preferred_element_type=F32
    )
    top, bottom = joined[0:8], joined[8:16]
    latent = jnp.concatenate(
        [top, pltpu.roll(top, 4, 0), bottom, pltpu.roll(bottom, 4, 0)], axis=1
    ).astype(BF16)

    head_value = jnp.concatenate(
        [
            jnp.where(even, jnp.dot(latent, uv_v[0], preferred_element_type=F32), 0.0),
            jnp.where(even, 0.0, jnp.dot(latent, uv_v[1], preferred_element_type=F32)),
        ],
        axis=1,
    )
    pairs = head_value + pltpu.roll(head_value, 7, 0)
    first = lax.broadcasted_iota(jnp.int32, (8, 1), 0) == 0
    flat = jnp.where(first, pairs, pltpu.roll(pairs, 7, 0)).astype(BF16)
    def share(z_pair, dy):
        group = ((y + dy) % 4) * 2 + z_pair
        columns = pl.ds(pl.multiple_of(group * 1024, 128), 1024)
        return group, jnp.dot(flat, w_p[:, columns], preferred_element_type=F32)

    def hand_out(z_pair, dy, group):
        for dx in (2, 1, 3, 0):
            for dz in (1, 0):
                peer = group * 8 + ((z + dz) % 2) * 4 + (x + dx) % 4
                if z_pair is own_pair and dy == 0 and dx == 0 and dz == 0:
                    tr[me, 0:2, :] = ts[me, 0:2, :]
                else:
                    remote(ts.at[peer, pl.ds(0, 2)], tr.at[me, pl.ds(0, 2)], 3, 9, {"kv": peer})

    def keep(group, term):
        for j in range(8):
            ts[group * 8 + j] = term[:, j * 128 : j * 128 + 128]

    order = [(z_pair, dy) for z_pair in (1 - own_pair, own_pair) for dy in (2, 1, 3, 0)]
    group, term = share(*order[0])
    keep(group, term)
    for k in range(8):
        later = share(*order[k + 1]) if k < 7 else None
        hand_out(*order[k], group)
        if later:
            group, term = later
            keep(group, term)
    take(tr.at[pl.ds(0, 63), pl.ds(0, 2)], recv_sem.at[9])
    result = jnp.sum(tr[:, 0:2, :], axis=0)
    out[0] = result[:, 0:112].astype(BF16)

    take(qs.at[pl.ds(0, 3), pl.ds(0, ASKED)], send_sem.at[0])
    take(qs.at[pl.ds(0, 60), pl.ds(0, ASKED)], send_sem.at[1])
    take(ob.at[pl.ds(0, 63), pl.ds(0, SENT)], send_sem.at[2])
    take(ts.at[pl.ds(0, 63), pl.ds(0, 2)], send_sem.at[3])


def body(q_nope, q_rope, uk, uv, out_w, cache, new_rows, context):
    hbm = pl.BlockSpec(memory_space=pltpu.HBM)
    result = pl.pallas_call(
        kernel,
        out_shape=pltpu.VMEM((1, STEPS, 112), BF16),
        in_specs=[hbm] * 8,
        out_specs=pl.BlockSpec(memory_space=pltpu.VMEM),
        scratch_shapes=[
            pltpu.VMEM((2, 1, 2, 128), BF16),
            pltpu.VMEM((2, 1, 2, ROPE), BF16),
            pltpu.VMEM((2, 128, LAT), BF16),
            pltpu.VMEM((2, LAT, 128), BF16),
            pltpu.VMEM((256, 7168), BF16),
            pltpu.VMEM((256, 8192), BF16),
            pltpu.VMEM((1, 2, WIDE), BF16),
            pltpu.VMEM((1, 1), jnp.int32),
            pltpu.VMEM((8, 128), F32),
            pltpu.VMEM((64, 32, 128), BF16),
            pltpu.VMEM((256, WIDE_PAD), F32),
            pltpu.VMEM((WIDE_PAD, 2048), BF16),
            pltpu.VMEM((2048, LAT), BF16),
            pltpu.VMEM((128, 2048), F32),
            pltpu.VMEM((256, LAT), F32),
            pltpu.VMEM((256, 128), F32),
            pltpu.VMEM((64, 32, 128), BF16),
            pltpu.VMEM((64, 32, 128), BF16),
            pltpu.VMEM((128, 1024), BF16),
            pltpu.VMEM((64, 8, 128), F32),
            pltpu.VMEM((64, 8, 128), F32),
            pltpu.SemaphoreType.DMA((8,)),
            pltpu.SemaphoreType.DMA((4,)),
            pltpu.SemaphoreType.DMA((10,)),
        ],
        compiler_params=pltpu.CompilerParams(
            collective_id=0, has_side_effects=True, vmem_limit_bytes=60 << 20
        ),
    )(q_nope, q_rope, uk, uv, out_w, jnp.swapaxes(cache, 1, 2), jnp.swapaxes(new_rows, 0, 1), context.reshape(1, 1))
    return jnp.swapaxes(result, 0, 1)


def solution(mesh):
    in_specs = (
        P(None, "req", "kv", None),
        P(None, "req", "kv", None),
        P("kv", None, None),
        P("kv", None, None),
        P("kv", None),
        P("req", "kv", None),
        P(None, "req", None),
        P("req"),
    )
    return jax.shard_map(body, mesh=mesh, in_specs=in_specs, out_specs=P(None, "req", "kv"), check_vma=False)
```

```python
import functools
import math

import jax
import jax.numpy as jnp
from jax import lax
from jax.experimental import pallas as pl
from jax.experimental.pallas import tpu as pltpu
from jax.sharding import PartitionSpec as P

MESH = pl.DeviceIdType.MESH
F32 = jnp.float32
BF16 = jnp.bfloat16

SIDE = 4
HOLD = 2
STEPS = 2
ROWS = HOLD * STEPS
LAT = 512
ROPE = 64
WIDE = LAT + ROPE
WIDE_PAD = 640
NEVER = -1e30
ASKED = 20
SENT = 18

RING = [(dy, dx) for dy in range(SIDE) for dx in range(SIDE) if dy or dx]
RING.sort(key=lambda d: -(min(d[0], SIDE - d[0]) + min(d[1], SIDE - d[1])))


def split(value):
    high = value.astype(BF16).astype(F32)
    return high, (value - high).astype(BF16).astype(F32)


def with_stats(peak, total, rows):
    lane = lax.broadcasted_iota(jnp.int32, (rows, 128), 1)
    row = lax.broadcasted_iota(jnp.int32, (rows, 128), 0) % ROWS
    result = jnp.zeros((rows, 128), F32)
    for at, part in enumerate((*split(peak), *split(total))):
        result = jnp.where(lane == row + at * ROWS, part, result)
    return result


def kernel(
    q_nope, q_rope, uk, uv, out_w, cache, new_rows, context, out,
    qn_v, qr_v, uk_v, uv_v, w_v, w_p, new_v, ctx_v, qx, qs, q_all, keys, latents, scores, vals, stats, ob, rb, spread, ts, tr,
    load_sem, send_sem, recv_sem,
):
    me = lax.axis_index("kv")
    y, z, x = me // 16, (me // 4) % 4, me % 4
    in_plane = [((y + dy) % 4, (x + dx) % 4) for dy, dx in RING]
    own_pair = z // 2
    in_line = [3 - 3 * own_pair, 2 - own_pair, z + 1 - 2 * (z % 2)]

    def plane_id(peer):
        return {"kv": peer[0] * 16 + z * 4 + peer[1]}

    def line_id(peer):
        return {"kv": y * 16 + peer * 4 + x}

    loads = [
        pltpu.make_async_copy(src, dst, load_sem.at[k])
        for k, (src, dst) in enumerate(
            [(q_nope, qn_v), (q_rope, qr_v), (uk, uk_v), (context, ctx_v), (new_rows, new_v), (cache.at[0], keys.at[pl.ds(0, WIDE)]), (uv.at[0], uv_v.at[:, pl.ds(0, 128)]), (out_w, w_v), (uv.at[1], uv_v.at[:, pl.ds(128, 128)])]
        )
    ]
    barrier = pltpu.get_barrier_semaphore()
    for peer in in_plane[:5]:
        pl.semaphore_signal(barrier, inc=1, device_id=plane_id(peer), device_id_type=MESH)
    for peer in in_line:
        pl.semaphore_signal(barrier, inc=1, device_id=line_id(peer), device_id_type=MESH)
    for peer in in_plane[5:]:
        pl.semaphore_signal(barrier, inc=1, device_id=plane_id(peer), device_id_type=MESH)
    for load in loads[:3]:
        load.start()
    for load in loads[3:]:
        load.start()
    l_qn, l_qr, l_uk, l_ctx, l_new, l_cache, l_uv, l_w, l_uv2 = loads

    l_qn.wait()
    l_qr.wait()
    l_uk.wait()
    low_half = lax.broadcasted_iota(jnp.int32, (8, 1), 0) < 4

    def halves(left, right):
        return (
            jnp.where(low_half, left, pltpu.roll(right, 4, 0)),
            jnp.where(low_half, pltpu.roll(left, 4, 0), right),
        )

    qx[...] = jnp.zeros((8, 128), F32)
    for step in range(STEPS):
        qx[step * 2 : step * 2 + 2, :] = qn_v[step, 0].astype(F32)
    lhs = qx[...].astype(BF16)
    even = lax.broadcasted_iota(jnp.int32, (8, 1), 0) % 2 == 0
    lat = jnp.where(
        even,
        jnp.dot(lhs, uk_v[0], preferred_element_type=F32),
        jnp.dot(lhs, uk_v[1], preferred_element_type=F32),
    )
    quarters = [lat[:, k * 128 : k * 128 + 128] for k in range(4)]
    qs[me, 0:16, :] = jnp.concatenate(
        [halves(*quarters[:2])[0], halves(*quarters[2:])[0]], axis=0
    ).astype(BF16)
    lane = lax.broadcasted_iota(jnp.int32, (2, ROPE), 1)
    for step in range(STEPS):
        flag = jnp.where(lane == step, 1.0, 0.0).astype(F32)
        qx[step * 2 : step * 2 + 2, :] = jnp.concatenate([qr_v[step, 0].astype(F32), flag], axis=1)
    tail = qx[...]
    qs[me, 16:32, :] = jnp.concatenate([tail, tail], axis=0).astype(BF16)

    pl.semaphore_wait(barrier, len(in_plane) + len(in_line))

    def remote(src, dst, sent, arrived, device):
        copy = pltpu.make_async_remote_copy(
            src_ref=src,
            dst_ref=dst,
            send_sem=send_sem.at[sent],
            recv_sem=recv_sem.at[arrived],
            device_id=device,
            device_id_type=MESH,
        )
        copy.start()

    def take(ref, sem):
        pltpu.make_async_copy(ref, ref, sem).wait()

    def slab(owner_z):
        return qs.at[y * 16 + owner_z * 4 + x, pl.ds(0, ASKED)]

    for peer in in_line:
        remote(slab(z), slab(z), 0, z, line_id(peer))
    for peer in in_plane:
        remote(slab(z), slab(z), 1, 4, plane_id(peer))

    l_ctx.wait()
    l_new.wait()
    l_cache.wait()
    length = ctx_v[...]
    rows = jnp.concatenate([new_v[0].astype(F32), jnp.zeros((STEPS, WIDE_PAD - WIDE), F32)], axis=1)
    appended = jnp.concatenate([rows, jnp.zeros((8 - STEPS, WIDE_PAD), F32)], axis=0).T
    row = lax.broadcasted_iota(jnp.int32, (WIDE_PAD - WIDE, 1), 0)

    def prepare(k, _):
        here = pl.ds(pl.multiple_of(k * 256, 256), 256)
        token = (lax.broadcasted_iota(jnp.int32, (1, 256), 1) + k * 256) * 64 + me
        block = keys[0:WIDE, here].astype(F32)
        for step in range(STEPS):
            block = jnp.where(token == length + step, appended[0:WIDE, step : step + 1], block)
        keys[0:WIDE, here] = block.astype(BF16)
        latents[here, :] = block[0:LAT].astype(BF16).T
        mask = jnp.where((row < STEPS) & (token > length + row), NEVER, 0.0)
        keys[WIDE:, here] = mask.astype(BF16)
        return 0

    def unpack(z_pair):
        for to_y in range(4):
            for to_x in range(4):
                owner = to_y * 16 + z_pair * 8 + to_x
                parts = [[qs[owner + j, k * 8 : k * 8 + 8, :].astype(F32) for k in range(3)] for j in (0, 4)]
                eight = pl.ds(pl.multiple_of(z_pair * 128 + (to_y * 4 + to_x) * 8, 8), 8)
                for k in range(3):
                    pieces = halves(parts[0][k], parts[1][k])
                    q_all[eight, k * 256 : k * 256 + 128] = pieces[0]
                    if k < 2:
                        q_all[eight, k * 256 + 128 : k * 256 + 256] = pieces[1]

    done = 0
    for k, chunks in ((2, 2), (1, 1), (0, 1)):
        lax.fori_loop(done, done + chunks, prepare, 0)
        done += chunks
        take(slab(in_line[k]), recv_sem.at[in_line[k]])
        for peer in in_plane:
            remote(slab(in_line[k]), slab(in_line[k]), 1, 7 - k, plane_id(peer))
    lax.fori_loop(done, 8, prepare, 0)
    column = lax.broadcasted_iota(jnp.int32, (128, 1024), 1) // 16
    place = lax.broadcasted_iota(jnp.int32, (128, 1024), 0)
    spread[...] = jnp.where(column == place, 1.0, 0.0).astype(BF16)

    scale = math.log2(math.e) * (128 + ROPE) ** -0.5

    def attend(z_pair):
        half = pl.ds(pl.multiple_of(z_pair * 128, 128), 128)
        queries = q_all[half, :].astype(BF16)
        peak = None
        for k in range(4):
            tiles = jnp.dot(queries, keys[:, k * 512 : k * 512 + 512], preferred_element_type=F32)
            scores[:, k * 512 : k * 512 + 512] = tiles
            for j in range(4):
                tile = tiles[:, j * 128 : j * 128 + 128]
                peak = tile if peak is None else jnp.maximum(peak, tile)
        high, low = split(jnp.max(peak, axis=1, keepdims=True) * scale)
        peak = high + low
        total = jnp.zeros((128, 128), F32)
        value = jnp.zeros((128, LAT), F32)
        for k in range(4):
            expo = jnp.exp2(scores[:, k * 512 : k * 512 + 512] * scale - peak)
            for j in range(4):
                total = total + expo[:, j * 128 : j * 128 + 128]
            value = value + jnp.dot(
                expo.astype(BF16), latents[k * 512 : k * 512 + 512, :], preferred_element_type=F32
            )
        vals[half, :] = value
        note = with_stats(peak, jnp.sum(total, axis=1, keepdims=True), 128)
        note = note + pltpu.roll(note, 1, 0)
        stats[half, :] = note + pltpu.roll(note, 2, 0)

    def deliver(z_pair):
        for dy, dx in (*RING, (0, 0)):
            to_y, to_x = (y + dy) % 4, (x + dx) % 4
            eight = pl.ds(pl.multiple_of(z_pair * 128 + (to_y * 4 + to_x) * 8, 8), 8)
            quarters = [vals[eight, k * 128 : k * 128 + 128] for k in range(4)]
            first, second = zip(halves(*quarters[:2]), halves(*quarters[2:]))
            note = stats[eight, :]
            for j, (rows, shift) in enumerate(((first, 5), (second, 1))):
                peer = to_y * 16 + (z_pair * 2 + j) * 4 + to_x
                ob[peer, 0:16, :] = jnp.concatenate(rows, axis=0).astype(BF16)
                moved = pltpu.roll(note, shift, 0)
                ob[peer, 16:32, :] = jnp.concatenate([moved, moved], axis=0).astype(BF16)
            for j in (1, 0):
                peer = to_y * 16 + (z_pair * 2 + (z + j) % 2) * 4 + to_x
                if z_pair is own_pair and dy == 0 and dx == 0 and j == 0:
                    rb[me] = ob[me]
                else:
                    remote(ob.at[peer, pl.ds(0, SENT)], rb.at[me, pl.ds(0, SENT)], 2, 8, {"kv": peer})

    def arrived(k):
        take(qs.at[pl.ds(0, 15), pl.ds(0, ASKED)], recv_sem.at[4 + k])

    arrived(0)
    arrived(1)
    unpack(own_pair)
    attend(own_pair)
    arrived(2)
    arrived(3)
    unpack(1 - own_pair)
    attend(1 - own_pair)
    deliver(1 - own_pair)
    deliver(own_pair)
    l_uv.wait()
    l_uv2.wait()
    l_w.wait()

    def align(group, _):
        columns = w_v[:, pl.ds(pl.multiple_of(group * 896, 128), 896)]
        gap = jnp.zeros((256, 16), BF16)
        w_p[:, pl.ds(pl.multiple_of(group * 1024, 128), 1024)] = jnp.concatenate(
            [piece for j in range(8) for piece in (columns[:, j * 112 : j * 112 + 112], gap)], axis=1
        )
        return 0

    lax.fori_loop(0, 8, align, 0)
    take(rb.at[pl.ds(0, 63), pl.ds(0, SENT)], recv_sem.at[8])
    notes = jnp.concatenate(
        [rb[k, 16:18, :].astype(F32)[0:1] for k in range(64)] + [jnp.zeros((64, 128), F32)], axis=0
    ).T
    known = lax.broadcasted_iota(jnp.int32, (ROWS, 128), 1) < 64
    peak = jnp.where(known, notes[0:4] + notes[4:8], -3e38)
    factor = jnp.where(known, jnp.exp2(peak - jnp.max(peak, axis=1, keepdims=True)), 0.0)
    whole = jnp.sum(factor * (notes[8:12] + notes[12:16]), axis=1, keepdims=True)
    factor = factor / whole
    factor = jnp.concatenate([factor, factor], axis=0).astype(BF16)
    factor = jnp.dot(factor, spread[...], preferred_element_type=F32)
    column = lax.broadcasted_iota(jnp.int32, (16, 1024), 1) % 16
    place = lax.broadcasted_iota(jnp.int32, (16, 1024), 0)
    factor = jnp.where(column == place, jnp.concatenate([factor, factor], axis=0), 0.0).astype(BF16)
    joined = jnp.dot(
        factor, rb[:, 0:16, :].reshape(1024, 128), preferred_element_type=F32
    )
    top, bottom = joined[0:8], joined[8:16]
    latent = jnp.concatenate(
        [top, pltpu.roll(top, 4, 0), bottom, pltpu.roll(bottom, 4, 0)], axis=1
    ).astype(BF16)

    own_head = (lax.broadcasted_iota(jnp.int32, (8, 256), 1) < 128) == even
    head_value = jnp.where(own_head, jnp.dot(latent, uv_v[...], preferred_element_type=F32), 0.0)
    pairs = head_value + pltpu.roll(head_value, 7, 0)
    first = lax.broadcasted_iota(jnp.int32, (8, 1), 0) == 0
    flat = jnp.where(first, pairs, pltpu.roll(pairs, 7, 0)).astype(BF16)
    def share(z_pair, dy):
        group = ((y + dy) % 4) * 2 + z_pair
        columns = pl.ds(pl.multiple_of(group * 1024, 128), 1024)
        return group, jnp.dot(flat, w_p[:, columns], preferred_element_type=F32)

    def hand_out(z_pair, dy, group):
        for dx in (2, 1, 3, 0):
            for dz in (1, 0):
                peer = group * 8 + ((z + dz) % 2) * 4 + (x + dx) % 4
                if z_pair is own_pair and dy == 0 and dx == 0 and dz == 0:
                    tr[me, 0:2, :] = ts[me, 0:2, :]
                else:
                    remote(ts.at[peer, pl.ds(0, 2)], tr.at[me, pl.ds(0, 2)], 3, 9, {"kv": peer})

    def keep(group, term):
        for j in range(8):
            ts[group * 8 + j] = term[:, j * 128 : j * 128 + 128]

    order = [(z_pair, dy) for z_pair in (1 - own_pair, own_pair) for dy in (2, 1, 3, 0)]
    group, term = share(*order[0])
    keep(group, term)
    for k in range(8):
        later = share(*order[k + 1]) if k < 7 else None
        hand_out(*order[k], group)
        if later:
            group, term = later
            keep(group, term)
    take(tr.at[pl.ds(0, 63), pl.ds(0, 2)], recv_sem.at[9])
    result = jnp.sum(tr[:, 0:2, :], axis=0)
    out[0] = result[:, 0:112].astype(BF16)

    take(qs.at[pl.ds(0, 3), pl.ds(0, ASKED)], send_sem.at[0])
    take(qs.at[pl.ds(0, 60), pl.ds(0, ASKED)], send_sem.at[1])
    take(ob.at[pl.ds(0, 63), pl.ds(0, SENT)], send_sem.at[2])
    take(ts.at[pl.ds(0, 63), pl.ds(0, 2)], send_sem.at[3])


def body(q_nope, q_rope, uk, uv, out_w, cache, new_rows, context):
    hbm = pl.BlockSpec(memory_space=pltpu.HBM)
    result = pl.pallas_call(
        kernel,
        out_shape=pltpu.VMEM((1, STEPS, 112), BF16),
        in_specs=[hbm] * 8,
        out_specs=pl.BlockSpec(memory_space=pltpu.VMEM),
        scratch_shapes=[
            pltpu.VMEM((2, 1, 2, 128), BF16),
            pltpu.VMEM((2, 1, 2, ROPE), BF16),
            pltpu.VMEM((2, 128, LAT), BF16),
            pltpu.VMEM((LAT, 256), BF16),
            pltpu.VMEM((256, 7168), BF16),
            pltpu.VMEM((256, 8192), BF16),
            pltpu.VMEM((1, 2, WIDE), BF16),
            pltpu.VMEM((1, 1), jnp.int32),
            pltpu.VMEM((8, 128), F32),
            pltpu.VMEM((64, 32, 128), BF16),
            pltpu.VMEM((256, WIDE_PAD), F32),
            pltpu.VMEM((WIDE_PAD, 2048), BF16),
            pltpu.VMEM((2048, LAT), BF16),
            pltpu.VMEM((128, 2048), F32),
            pltpu.VMEM((256, LAT), F32),
            pltpu.VMEM((256, 128), F32),
            pltpu.VMEM((64, 32, 128), BF16),
            pltpu.VMEM((64, 32, 128), BF16),
            pltpu.VMEM((128, 1024), BF16),
            pltpu.VMEM((64, 8, 128), F32),
            pltpu.VMEM((64, 8, 128), F32),
            pltpu.SemaphoreType.DMA((9,)),
            pltpu.SemaphoreType.DMA((4,)),
            pltpu.SemaphoreType.DMA((10,)),
        ],
        compiler_params=pltpu.CompilerParams(
            collective_id=0, has_side_effects=True, vmem_limit_bytes=60 << 20
        ),
    )(q_nope, q_rope, uk, uv, out_w, jnp.swapaxes(cache, 1, 2), jnp.swapaxes(new_rows, 0, 1), context.reshape(1, 1))
    return jnp.swapaxes(result, 0, 1)


def solution(mesh):
    in_specs = (
        P(None, "req", "kv", None),
        P(None, "req", "kv", None),
        P("kv", None, None),
        P("kv", None, None),
        P("kv", None),
        P("req", "kv", None),
        P(None, "req", None),
        P("req"),
    )
    return jax.shard_map(body, mesh=mesh, in_specs=in_specs, out_specs=P(None, "req", "kv"), check_vma=False)
```

```python
import functools
import math

import jax
import jax.numpy as jnp
from jax import lax
from jax.experimental import pallas as pl
from jax.experimental.pallas import tpu as pltpu
from jax.sharding import PartitionSpec as P

MESH = pl.DeviceIdType.MESH
F32 = jnp.float32
BF16 = jnp.bfloat16

SIDE = 4
HOLD = 2
STEPS = 2
ROWS = HOLD * STEPS
LAT = 512
ROPE = 64
WIDE = LAT + ROPE
WIDE_PAD = 640
NEVER = -1e30
ASKED = 20
SENT = 18

RING = [(dy, dx) for dy in range(SIDE) for dx in range(SIDE) if dy or dx]
RING.sort(key=lambda d: -(min(d[0], SIDE - d[0]) + min(d[1], SIDE - d[1])))


def split(value):
    high = value.astype(BF16).astype(F32)
    return high, (value - high).astype(BF16).astype(F32)


def with_stats(peak, total, rows):
    lane = lax.broadcasted_iota(jnp.int32, (rows, 128), 1)
    row = lax.broadcasted_iota(jnp.int32, (rows, 128), 0) % ROWS
    result = jnp.zeros((rows, 128), F32)
    for at, part in enumerate((*split(peak), *split(total))):
        result = jnp.where(lane == row + at * ROWS, part, result)
    return result


def kernel(
    q_nope, q_rope, uk, uv, out_w, cache, new_rows, context, out,
    qn_v, qr_v, uk_v, uv_v, w_v, w_p, new_v, ctx_v, qx, qs, q_all, keys, latents, scores, vals, stats, ob, rb, spread, ts, tr,
    load_sem, send_sem, recv_sem,
):
    me = lax.axis_index("kv")
    y, z, x = me // 16, (me // 4) % 4, me % 4
    in_plane = [((y + dy) % 4, (x + dx) % 4) for dy, dx in RING]
    own_pair = z // 2
    in_line = [3 - 3 * own_pair, 2 - own_pair, z + 1 - 2 * (z % 2)]

    def plane_id(peer):
        return {"kv": peer[0] * 16 + z * 4 + peer[1]}

    def line_id(peer):
        return {"kv": y * 16 + peer * 4 + x}

    loads = [
        pltpu.make_async_copy(src, dst, load_sem.at[k])
        for k, (src, dst) in enumerate(
            [(q_nope, qn_v), (q_rope, qr_v), (uk, uk_v), (context, ctx_v), (new_rows, new_v), (cache.at[0], keys.at[pl.ds(0, WIDE)]), (uv, uv_v), (out_w, w_v)]
        )
    ]
    barrier = pltpu.get_barrier_semaphore()
    for peer in in_plane[:5]:
        pl.semaphore_signal(barrier, inc=1, device_id=plane_id(peer), device_id_type=MESH)
    for peer in in_line:
        pl.semaphore_signal(barrier, inc=1, device_id=line_id(peer), device_id_type=MESH)
    for peer in in_plane[5:]:
        pl.semaphore_signal(barrier, inc=1, device_id=plane_id(peer), device_id_type=MESH)
    for load in loads[:3]:
        load.start()
    for load in loads[3:]:
        load.start()
    l_qn, l_qr, l_uk, l_ctx, l_new, l_cache, l_uv, l_w = loads

    l_qn.wait()
    l_qr.wait()
    l_uk.wait()
    low_half = lax.broadcasted_iota(jnp.int32, (8, 1), 0) < 4

    def halves(left, right):
        return (
            jnp.where(low_half, left, pltpu.roll(right, 4, 0)),
            jnp.where(low_half, pltpu.roll(left, 4, 0), right),
        )

    qx[...] = jnp.zeros((8, 128), F32)
    for step in range(STEPS):
        qx[step * 2 : step * 2 + 2, :] = qn_v[step, 0].astype(F32)
    lhs = qx[...].astype(BF16)
    even = lax.broadcasted_iota(jnp.int32, (8, 1), 0) % 2 == 0
    lat = jnp.where(
        even,
        jnp.dot(lhs, uk_v[0], preferred_element_type=F32),
        jnp.dot(lhs, uk_v[1], preferred_element_type=F32),
    )
    quarters = [lat[:, k * 128 : k * 128 + 128] for k in range(4)]
    qs[me, 0:16, :] = jnp.concatenate(
        [halves(*quarters[:2])[0], halves(*quarters[2:])[0]], axis=0
    ).astype(BF16)
    lane = lax.broadcasted_iota(jnp.int32, (2, ROPE), 1)
    for step in range(STEPS):
        flag = jnp.where(lane == step, 1.0, 0.0).astype(F32)
        qx[step * 2 : step * 2 + 2, :] = jnp.concatenate([qr_v[step, 0].astype(F32), flag], axis=1)
    tail = qx[...]
    qs[me, 16:32, :] = jnp.concatenate([tail, tail], axis=0).astype(BF16)

    pl.semaphore_wait(barrier, len(in_plane) + len(in_line))

    def remote(src, dst, sent, arrived, device):
        copy = pltpu.make_async_remote_copy(
            src_ref=src,
            dst_ref=dst,
            send_sem=send_sem.at[sent],
            recv_sem=recv_sem.at[arrived],
            device_id=device,
            device_id_type=MESH,
        )
        copy.start()

    def take(ref, sem):
        pltpu.make_async_copy(ref, ref, sem).wait()

    def slab(owner_z):
        return qs.at[y * 16 + owner_z * 4 + x, pl.ds(0, ASKED)]

    for peer in in_line:
        remote(slab(z), slab(z), 0, z, line_id(peer))
    for peer in in_plane:
        remote(slab(z), slab(z), 1, 4, plane_id(peer))

    l_ctx.wait()
    l_new.wait()
    l_cache.wait()
    length = ctx_v[...]
    rows = jnp.concatenate([new_v[0].astype(F32), jnp.zeros((STEPS, WIDE_PAD - WIDE), F32)], axis=1)
    appended = jnp.concatenate([rows, jnp.zeros((8 - STEPS, WIDE_PAD), F32)], axis=0).T
    row = lax.broadcasted_iota(jnp.int32, (WIDE_PAD - WIDE, 1), 0)

    def prepare(k, _):
        here = pl.ds(pl.multiple_of(k * 256, 256), 256)
        token = (lax.broadcasted_iota(jnp.int32, (1, 256), 1) + k * 256) * 64 + me
        block = keys[0:WIDE, here].astype(F32)
        for step in range(STEPS):
            block = jnp.where(token == length + step, appended[0:WIDE, step : step + 1], block)
        keys[0:WIDE, here] = block.astype(BF16)
        latents[here, :] = block[0:LAT].astype(BF16).T
        mask = jnp.where((row < STEPS) & (token > length + row), NEVER, 0.0)
        keys[WIDE:, here] = mask.astype(BF16)
        return 0

    def unpack(z_pair):
        for to_y in range(4):
            for to_x in range(4):
                owner = to_y * 16 + z_pair * 8 + to_x
                parts = [[qs[owner + j, k * 8 : k * 8 + 8, :].astype(F32) for k in range(3)] for j in (0, 4)]
                eight = pl.ds(pl.multiple_of(z_pair * 128 + (to_y * 4 + to_x) * 8, 8), 8)
                for k in range(3):
                    pieces = halves(parts[0][k], parts[1][k])
                    q_all[eight, k * 256 : k * 256 + 128] = pieces[0]
                    if k < 2:
                        q_all[eight, k * 256 + 128 : k * 256 + 256] = pieces[1]

    done = 0
    for k, chunks in ((2, 2), (1, 1), (0, 1)):
        lax.fori_loop(done, done + chunks, prepare, 0)
        done += chunks
        take(slab(in_line[k]), recv_sem.at[in_line[k]])
        for peer in in_plane:
            remote(slab(in_line[k]), slab(in_line[k]), 1, 7 - k, plane_id(peer))
    lax.fori_loop(done, 8, prepare, 0)
    column = lax.broadcasted_iota(jnp.int32, (128, 1024), 1) // 16
    place = lax.broadcasted_iota(jnp.int32, (128, 1024), 0)
    spread[...] = jnp.where(column == place, 1.0, 0.0).astype(BF16)

    scale = math.log2(math.e) * (128 + ROPE) ** -0.5

    def attend(z_pair):
        half = pl.ds(pl.multiple_of(z_pair * 128, 128), 128)
        queries = q_all[half, :].astype(BF16)
        peak = None
        for k in range(2):
            tiles = jnp.dot(queries, keys[:, k * 1024 : k * 1024 + 1024], preferred_element_type=F32)
            scores[:, k * 1024 : k * 1024 + 1024] = tiles
            for j in range(8):
                tile = tiles[:, j * 128 : j * 128 + 128]
                peak = tile if peak is None else jnp.maximum(peak, tile)
        high, low = split(jnp.max(peak, axis=1, keepdims=True) * scale)
        peak = high + low
        total = jnp.zeros((128, 128), F32)
        value = jnp.zeros((128, LAT), F32)
        for k in range(4):
            expo = jnp.exp2(scores[:, k * 512 : k * 512 + 512] * scale - peak)
            for j in range(4):
                total = total + expo[:, j * 128 : j * 128 + 128]
            value = value + jnp.dot(
                expo.astype(BF16), latents[k * 512 : k * 512 + 512, :], preferred_element_type=F32
            )
        vals[half, :] = value
        stats[half, :] = with_stats(peak, jnp.sum(total, axis=1, keepdims=True), 128)

    def deliver(z_pair):
        for dy, dx in (*RING, (0, 0)):
            to_y, to_x = (y + dy) % 4, (x + dx) % 4
            eight = pl.ds(pl.multiple_of(z_pair * 128 + (to_y * 4 + to_x) * 8, 8), 8)
            quarters = [vals[eight, k * 128 : k * 128 + 128] for k in range(4)]
            first, second = zip(halves(*quarters[:2]), halves(*quarters[2:]))
            note = stats[eight, :]
            note = note + pltpu.roll(note, 1, 0)
            note = note + pltpu.roll(note, 2, 0)
            for j, (rows, shift) in enumerate(((first, 5), (second, 1))):
                peer = to_y * 16 + (z_pair * 2 + j) * 4 + to_x
                ob[peer, 0:16, :] = jnp.concatenate(rows, axis=0).astype(BF16)
                moved = pltpu.roll(note, shift, 0)
                ob[peer, 16:32, :] = jnp.concatenate([moved, moved], axis=0).astype(BF16)
            for j in (1, 0):
                peer = to_y * 16 + (z_pair * 2 + (z + j) % 2) * 4 + to_x
                if z_pair is own_pair and dy == 0 and dx == 0 and j == 0:
                    rb[me] = ob[me]
                else:
                    remote(ob.at[peer, pl.ds(0, SENT)], rb.at[me, pl.ds(0, SENT)], 2, 8, {"kv": peer})

    def arrived(k):
        take(qs.at[pl.ds(0, 15), pl.ds(0, ASKED)], recv_sem.at[4 + k])

    arrived(0)
    arrived(1)
    unpack(own_pair)
    attend(own_pair)
    arrived(2)
    arrived(3)
    unpack(1 - own_pair)
    attend(1 - own_pair)
    deliver(1 - own_pair)
    deliver(own_pair)
    l_uv.wait()
    l_w.wait()

    def align(group, _):
        columns = w_v[:, pl.ds(pl.multiple_of(group * 896, 128), 896)]
        gap = jnp.zeros((256, 16), BF16)
        w_p[:, pl.ds(pl.multiple_of(group * 1024, 128), 1024)] = jnp.concatenate(
            [piece for j in range(8) for piece in (columns[:, j * 112 : j * 112 + 112], gap)], axis=1
        )
        return 0

    lax.fori_loop(0, 8, align, 0)
    take(rb.at[pl.ds(0, 63), pl.ds(0, SENT)], recv_sem.at[8])
    notes = jnp.concatenate(
        [rb[k, 16:18, :].astype(F32)[0:1] for k in range(64)] + [jnp.zeros((64, 128), F32)], axis=0
    ).T
    known = lax.broadcasted_iota(jnp.int32, (ROWS, 128), 1) < 64
    peak = jnp.where(known, notes[0:4] + notes[4:8], -3e38)
    factor = jnp.where(known, jnp.exp2(peak - jnp.max(peak, axis=1, keepdims=True)), 0.0)
    whole = jnp.sum(factor * (notes[8:12] + notes[12:16]), axis=1, keepdims=True)
    factor = factor / whole
    factor = jnp.concatenate([factor, factor], axis=0).astype(BF16)
    factor = jnp.dot(factor, spread[...], preferred_element_type=F32)
    column = lax.broadcasted_iota(jnp.int32, (16, 1024), 1) % 16
    place = lax.broadcasted_iota(jnp.int32, (16, 1024), 0)
    factor = jnp.where(column == place, jnp.concatenate([factor, factor], axis=0), 0.0).astype(BF16)
    joined = jnp.dot(
        factor, rb[:, 0:16, :].reshape(1024, 128), preferred_element_type=F32
    )
    top, bottom = joined[0:8], joined[8:16]
    latent = jnp.concatenate(
        [top, pltpu.roll(top, 4, 0), bottom, pltpu.roll(bottom, 4, 0)], axis=1
    ).astype(BF16)

    head_value = jnp.concatenate(
        [
            jnp.where(even, jnp.dot(latent, uv_v[0], preferred_element_type=F32), 0.0),
            jnp.where(even, 0.0, jnp.dot(latent, uv_v[1], preferred_element_type=F32)),
        ],
        axis=1,
    )
    pairs = head_value + pltpu.roll(head_value, 7, 0)
    first = lax.broadcasted_iota(jnp.int32, (8, 1), 0) == 0
    flat = jnp.where(first, pairs, pltpu.roll(pairs, 7, 0)).astype(BF16)
    def share(z_pair, dy):
        group = ((y + dy) % 4) * 2 + z_pair
        columns = pl.ds(pl.multiple_of(group * 1024, 128), 1024)
        return group, jnp.dot(flat, w_p[:, columns], preferred_element_type=F32)

    def hand_out(z_pair, dy, group):
        for dx in (2, 1, 3, 0):
            for dz in (1, 0):
                peer = group * 8 + ((z + dz) % 2) * 4 + (x + dx) % 4
                if z_pair is own_pair and dy == 0 and dx == 0 and dz == 0:
                    tr[me, 0:2, :] = ts[me, 0:2, :]
                else:
                    remote(ts.at[peer, pl.ds(0, 2)], tr.at[me, pl.ds(0, 2)], 3, 9, {"kv": peer})

    def keep(group, term):
        for j in range(8):
            ts[group * 8 + j] = term[:, j * 128 : j * 128 + 128]

    order = [(z_pair, dy) for z_pair in (1 - own_pair, own_pair) for dy in (2, 1, 3, 0)]
    group, term = share(*order[0])
    keep(group, term)
    for k in range(8):
        later = share(*order[k + 1]) if k < 7 else None
        hand_out(*order[k], group)
        if later:
            group, term = later
            keep(group, term)
    take(tr.at[pl.ds(0, 63), pl.ds(0, 2)], recv_sem.at[9])
    result = jnp.sum(tr[:, 0:2, :], axis=0)
    out[0] = result[:, 0:112].astype(BF16)

    take(qs.at[pl.ds(0, 3), pl.ds(0, ASKED)], send_sem.at[0])
    take(qs.at[pl.ds(0, 60), pl.ds(0, ASKED)], send_sem.at[1])
    take(ob.at[pl.ds(0, 63), pl.ds(0, SENT)], send_sem.at[2])
    take(ts.at[pl.ds(0, 63), pl.ds(0, 2)], send_sem.at[3])


def body(q_nope, q_rope, uk, uv, out_w, cache, new_rows, context):
    hbm = pl.BlockSpec(memory_space=pltpu.HBM)
    result = pl.pallas_call(
        kernel,
        out_shape=pltpu.VMEM((1, STEPS, 112), BF16),
        in_specs=[hbm] * 8,
        out_specs=pl.BlockSpec(memory_space=pltpu.VMEM),
        scratch_shapes=[
            pltpu.VMEM((2, 1, 2, 128), BF16),
            pltpu.VMEM((2, 1, 2, ROPE), BF16),
            pltpu.VMEM((2, 128, LAT), BF16),
            pltpu.VMEM((2, LAT, 128), BF16),
            pltpu.VMEM((256, 7168), BF16),
            pltpu.VMEM((256, 8192), BF16),
            pltpu.VMEM((1, 2, WIDE), BF16),
            pltpu.VMEM((1, 1), jnp.int32),
            pltpu.VMEM((8, 128), F32),
            pltpu.VMEM((64, 32, 128), BF16),
            pltpu.VMEM((256, WIDE_PAD), F32),
            pltpu.VMEM((WIDE_PAD, 2048), BF16),
            pltpu.VMEM((2048, LAT), BF16),
            pltpu.VMEM((128, 2048), F32),
            pltpu.VMEM((256, LAT), F32),
            pltpu.VMEM((256, 128), F32),
            pltpu.VMEM((64, 32, 128), BF16),
            pltpu.VMEM((64, 32, 128), BF16),
            pltpu.VMEM((128, 1024), BF16),
            pltpu.VMEM((64, 8, 128), F32),
            pltpu.VMEM((64, 8, 128), F32),
            pltpu.SemaphoreType.DMA((8,)),
            pltpu.SemaphoreType.DMA((4,)),
            pltpu.SemaphoreType.DMA((10,)),
        ],
        compiler_params=pltpu.CompilerParams(
            collective_id=0, has_side_effects=True, vmem_limit_bytes=60 << 20
        ),
    )(q_nope, q_rope, uk, uv, out_w, jnp.swapaxes(cache, 1, 2), jnp.swapaxes(new_rows, 0, 1), context.reshape(1, 1))
    return jnp.swapaxes(result, 0, 1)


def solution(mesh):
    in_specs = (
        P(None, "req", "kv", None),
        P(None, "req", "kv", None),
        P("kv", None, None),
        P("kv", None, None),
        P("kv", None),
        P("req", "kv", None),
        P(None, "req", None),
        P("req"),
    )
    return jax.shard_map(body, mesh=mesh, in_specs=in_specs, out_specs=P(None, "req", "kv"), check_vma=False)
```
